256 devices in a mesh: pool: 2 (over x_lo), ep: 128 (over y, x_hi, z, core).
Axes of the slice: x: 4 (x_hi: 2, x_lo: 2; x = x_hi * 2 + x_lo), y: 4, z: 8, core: 2. Of those that a mesh axis runs over, the one named last changes fastest.
Arguments:
- cache: bfloat16 [2, 256, 128, 576], P('pool', None, 'ep'), may hold values from -448 to 448, as said below
- cache_scale: bfloat16 [2, 256, 128, 4], P('pool', None, 'ep'), may hold values from 0.0006980896 to 0.0069885254
- lengths: int32 [2, 256], replicated, may hold values from 1 to 128, 10922 in all within a row
- assign: int32 [2, 256], replicated, may hold values from 0 to 255, each once within a row
- queries: bfloat16 [2, 256, 4, 64, 576], P('pool', 'ep'), may hold values from -360 to 360
- new_kv: bfloat16 [2, 256, 4, 576], P('pool', 'ep'), may hold values from -6 to 6
- hidden: bfloat16 [2, 256, 4, 3584], P('pool', 'ep'), may hold values from -6 to 6
- expert_ids: int32 [2, 256, 4, 8], P('pool', 'ep'), may hold values from 0 to 127, all different within a row; in each aligned block of 8 rows (0 to 7, 8 to 15, ..., all dimensions but the last counted through in order) at most 2 rows name the same one
- expert_weights: float32 [2, 256, 4, 8], P('pool', 'ep'), may hold values from 0.1 to 0.6
- gate_w: bfloat16 [128, 3584, 1024], P('ep', None, 'pool'), may hold values from -0.09375 to 0.09375
- up_w: bfloat16 [128, 3584, 1024], P('ep', None, 'pool'), may hold values from -0.09375 to 0.09375
- down_w: bfloat16 [128, 1024, 3584], P('ep', 'pool'), may hold values from -0.1875 to 0.1875
Outputs:
- context: bfloat16 [2, 256, 4, 64, 512], P('pool', 'ep')
- moe_out: bfloat16 [2, 256, 4, 3584], P('pool', 'ep')
The draws below stay inside these ranges and needn't reach their ends.
Inputs may be any that keep to these rules, and one draw needn't show every extreme that they name: `cache`: the first 512 entries of a row are stored values of a block-scaled format; the last 64 are plain keys. Each group's lengths sum to 10922 and one request has exactly 128. `assign`: each group's row is a permutation of the slots; slot v belongs to ep index v // 2. `expert_ids`: each token names 8 different experts. Within the rows of one device (aligned blocks of 8 tokens in the order group, slot, step) no expert is named more than 2 times, a bound that some block reaches.
All inputs are finite; a program needn't handle non-finite values.
Results may differ from the reference program's by a relative error of at most 0.0057.
Values may be sent and summed in bfloat16 or wider, within the bound.
No kernel may reach another device: no remote copies, remote signals or barrier semaphores. Data moves between devices by JAX's collectives and lax.ppermute only.
A program may use at most 128 MiB of HBM per device.

```python
import math
import jax
import jax.numpy as jnp
import numpy as np
from jax import lax

SLOT_DEV = 2
STEPS = 4
HEADS = 64
LAT = 512
ROPE = 64
QB = 128
D = 3584
FFE = 1024
TOP = 8
SLOTS = 256
LMAX = 128
EXPERTS = 128
CAP = 2
N_EP = 128


def draw_cache(key, part):
    key = jax.random.fold_in(key, 17)
    first, second = jax.random.split(key)
    stored = jax.random.uniform(first, (2, SLOTS, LMAX, LAT), jnp.float32, -448.0, 448.0)
    drawn = jnp.clip(jax.random.normal(second, (2, SLOTS, LMAX, ROPE), jnp.float32), -6.0, 6.0)
    return jnp.concatenate([stored, drawn], axis=-1).astype(jnp.bfloat16)


def draw_queries(key, part):
    key = jax.random.fold_in(key, 29)
    first = jax.random.fold_in(key, 0)
    values = jnp.clip(jax.random.normal(first, (2, SLOTS, STEPS, HEADS, LAT + ROPE), jnp.float32), -6.0, 6.0)
    return values.astype(jnp.bfloat16)


def steps_of(own_key, shape, cuts, smallest, top_value):
    def one(dim, shards_of):
        heights = jax.random.uniform(jax.random.fold_in(jax.random.fold_in(own_key, 6), dim), (shards_of,), jnp.float32, smallest / len(cuts), top_value / len(cuts))
        return jnp.repeat(jnp.exp(heights), shape[dim] // shards_of).reshape((-1,) + (1,) * (len(shape) - dim - 1))

    level = one(*cuts[0])
    for cut in cuts[1:]:
        level = level * one(*cut)
    return level


def split_up(number_of, total, limit, skew):
    weights = [(1 << 20) // math.isqrt(standing ** skew) + 1 for standing in range(2, number_of + 1)]
    rest, holding = total - limit - (number_of - 1), [1] * (number_of - 1)
    while rest > 0:
        free = [i for i in range(number_of - 1) if holding[i] < limit]
        whole, remaining = sum([weights[i] for i in free]), rest
        for i in free:
            addition = min(limit - holding[i], max(1, remaining * weights[i] // whole), rest)
            holding[i] = holding[i] + addition
            rest = rest - addition
    return np.array([limit] + holding)


def ragged_sizes(key, amount, total, most, skew):
    if amount == 2:
        one = jax.random.randint(key, (), max(1, total - most), min(most, total - 1) + 1)
        return jnp.stack([one, total - one])
    sizes = jnp.asarray(split_up(amount, total, most, skew), jnp.int32)
    twos = (amount - 1) // 2
    giver, receiver = sizes[1:1 + 2 * twos:2], sizes[2:2 + 2 * twos:2]
    room = jnp.minimum(giver - 1, most - receiver)
    shifted = jax.random.randint(jax.random.fold_in(key, 1), (twos,), 0, 1 << 20) % (room + 1)
    sizes = sizes.at[1:1 + 2 * twos:2].set(giver - shifted).at[2:2 + 2 * twos:2].set(receiver + shifted)
    return sizes[jax.random.permutation(jax.random.fold_in(key, 2), amount)]


def routed_block(key, own, number, rows, number_of, top, most, lean):
    sequence = jax.random.permutation(key, number_of)
    heavy_load, common = portions_of(number_of, rows * top, most, lean, True), portions_of(number_of, rows * top, most, lean, False)
    places = jnp.arange(number_of)

    def named(tallies, offset_by):
        used = int((tallies > 0).sum())
        fixed = max(1, used // 4)
        passed = fixed + (places - fixed + offset_by * (used - fixed)) % max(1, number_of - fixed)
        return jnp.zeros((number_of,), jnp.int32).at[sequence[jnp.where(places < fixed, places, passed)]].set(jnp.asarray(tallies, jnp.int32))

    tallies = jnp.where(number % 4 == 0, named(heavy_load, number // 4), named(common, number - number // 4 - 1))
    mixed = jax.random.permutation(jax.random.fold_in(own, 3), number_of)
    donor, receiver = mixed[0:number_of // 2 * 2:2], mixed[1:number_of // 2 * 2:2]
    margin = jnp.minimum(tallies[donor] - 1, most - tallies[receiver]) // 2
    margin = jnp.where((donor == sequence[0]) | (receiver == sequence[0]) | (tallies[receiver] == 0), 0, jnp.maximum(margin, 0))
    passed = jax.random.randint(jax.random.fold_in(own, 4), (number_of // 2,), 0, 1 << 20) % (margin + 1)
    tallies = tallies.at[donor].add(-passed).at[receiver].add(passed)
    members = jnp.searchsorted(jnp.cumsum(tallies), jnp.arange(rows * top), side="right").astype(jnp.int32)
    grid = members.reshape(top, rows).T
    grid = grid[jax.random.permutation(jax.random.fold_in(own, 1), rows)]
    offset_by = jax.random.randint(jax.random.fold_in(own, 2), (rows, 1), 0, top)
    return jnp.take_along_axis(grid, (jnp.arange(top)[None, :] + offset_by) % top, axis=1)


def portions_of(amount, total, reach, skew, full):
    loads = [(1 << 20) // math.isqrt(rank ** skew) + 1 for rank in range(1, amount + 1)]
    largest = reach if full else min(reach, max(-(-total // amount), total * loads[0] // sum(loads)))
    least = 1 if total - largest >= amount - 1 else 0
    given, rest = [largest] + [least] * (amount - 1), total - largest - least * (amount - 1)
    while rest > 0:
        movable = [i for i in range(1, amount) if given[i] < largest] or [i for i in range(1, amount) if given[i] < reach]
        pool, left = sum([loads[i] for i in movable]), rest
        for i in movable:
            addition = min(reach - given[i], max(1, left * loads[i] // pool), rest)
            given[i] = given[i] + addition
            rest = rest - addition
    return np.array(given)


def scatter_about(rng, extent, deviation, most, shards=(), held_as=jnp.bfloat16):
    factor_of = steps_of(rng, extent, shards, -0.22, 0.18) if shards else 1.0
    values = jax.random.normal(rng, extent, jnp.float32) * deviation * factor_of
    return jnp.minimum(jnp.maximum(values, -most), most).astype(held_as)


def setup_inputs(seed: int = 0) -> dict:
    key_list = jax.random.split(jax.random.key(seed), 13)
    cache = draw_cache(jax.random.fold_in(key_list[12], 71), 0)
    cache_scale = jnp.clip(jnp.exp(math.log(0.0069885254) - 2.3036774 * jax.random.uniform(key_list[1], (2, SLOTS, LMAX, LAT // QB), jnp.float32) ** steps_of(key_list[1], (2, SLOTS, LMAX, LAT // QB), ((0, 2), (2, 128)), -0.2, 0.2)), 0.0006980896, 0.0069885254).astype(jnp.bfloat16)
    lengths = jax.vmap(lambda own: ragged_sizes(own, SLOTS, SLOTS * LMAX // 3, LMAX, 2))(jax.random.split(key_list[2], 2)).reshape((2, SLOTS)).astype(jnp.int32)
    assign = jax.vmap(lambda own: jax.random.permutation(own, SLOTS))(jax.random.split(key_list[3], 2)).reshape((2, SLOTS)).astype(jnp.int32)
    queries = draw_queries(jax.random.fold_in(key_list[12], 71), 0)
    new_kv = scatter_about(key_list[5], (2, SLOTS, STEPS, LAT + ROPE), 1.0, 6.0, ((0, 2), (1, 128)))
    hidden = scatter_about(key_list[6], (2, SLOTS, STEPS, D), 1.0, 6.0, ((0, 2), (1, 128)))
    expert_ids_keys = jax.random.split(jax.random.fold_in(key_list[7], 1), 2 * SLOTS * STEPS // (SLOT_DEV * STEPS))
    expert_ids_turns = jax.random.permutation(jax.random.fold_in(key_list[7], 3), 2 * SLOTS * STEPS // (SLOT_DEV * STEPS))
    expert_ids = jax.vmap(lambda own, number: routed_block(jax.random.fold_in(key_list[7], 2), own, number, SLOT_DEV * STEPS, EXPERTS, TOP, CAP, 2))(expert_ids_keys, expert_ids_turns).reshape((2, SLOTS, STEPS, TOP))
    expert_weights = jnp.clip(0.1 + 0.5 * jax.random.uniform(key_list[8], (2, SLOTS, STEPS, TOP), jnp.float32) ** steps_of(key_list[8], (2, SLOTS, STEPS, TOP), ((0, 2), (1, 128)), -0.2, 0.2), 0.1, 0.6)
    gate_w = scatter_about(key_list[9], (EXPERTS, D, FFE), D ** -0.5, 0.09375, ((0, 128), (2, 2)))
    up_w = scatter_about(key_list[10], (EXPERTS, D, FFE), D ** -0.5, 0.09375, ((0, 128), (2, 2)))
    down_w = scatter_about(key_list[11], (EXPERTS, FFE, D), FFE ** -0.5, 0.1875, ((0, 128), (1, 2)))
    return {"cache": cache, "cache_scale": cache_scale, "lengths": lengths, "assign": assign, "queries": queries, "new_kv": new_kv, "hidden": hidden, "expert_ids": expert_ids, "expert_weights": expert_weights, "gate_w": gate_w, "up_w": up_w, "down_w": down_w}


SCORE_SCALE = 192.0 ** -0.5
NEGATIVE = -1.0e30


def attend_slot(inputs):
    query_rows, fresh_keys, values, scales, length = inputs
    blocks = LAT // QB
    query_full = query_rows.astype(jnp.float32)
    value_full = values.astype(jnp.float32)
    fresh_full = fresh_keys.astype(jnp.float32)
    scale_full = scales.astype(jnp.float32)
    query_latent = query_full[..., :LAT].reshape(STEPS, HEADS, blocks, QB)
    value_latent = value_full[:, :LAT].reshape(LMAX, blocks, QB)
    partial_value = jnp.einsum("shnc,pnc->shpn", query_latent, value_latent)
    score_cache = jnp.sum(partial_value * scale_full[None, None, :, :], axis=-1)
    score_cache = score_cache + jnp.einsum("shr,pr->shp", query_full[..., LAT:], value_full[:, LAT:])
    score_cache = score_cache * SCORE_SCALE
    position = jnp.arange(LMAX, dtype=jnp.int32)
    score_cache = jnp.where(position[None, None, :] < length, score_cache, NEGATIVE)
    score_fresh = jnp.einsum("shc,tc->sht", query_full, fresh_full) * SCORE_SCALE
    step_index = jnp.arange(STEPS, dtype=jnp.int32)
    allowed = step_index[None, None, :] <= step_index[:, None, None]
    score_fresh = jnp.where(allowed, score_fresh, NEGATIVE)
    row_max = jnp.maximum(jnp.max(score_cache, axis=-1), jnp.max(score_fresh, axis=-1))[..., None]
    exp_cache = jnp.exp(score_cache - row_max)
    exp_fresh = jnp.exp(score_fresh - row_max)
    summed = jnp.sum(exp_cache, axis=-1, keepdims=True) + jnp.sum(exp_fresh, axis=-1, keepdims=True)
    prob_cache = exp_cache / summed
    prob_fresh = exp_fresh / summed
    weight_cache = (prob_cache[..., None] * scale_full[None, None, :, :]).astype(jnp.bfloat16)
    weight_fresh = prob_fresh.astype(jnp.bfloat16)
    latent = jnp.einsum("shpn,pnc->shnc", weight_cache.astype(jnp.float32), value_latent).reshape(STEPS, HEADS, LAT)
    latent = latent + jnp.einsum("sht,tc->shc", weight_fresh.astype(jnp.float32), fresh_full[:, :LAT])
    return latent.astype(jnp.bfloat16)


def expert_apply(rows, gate_part, up_part, down_part):
    gate_val = jnp.dot(rows, gate_part, preferred_element_type=jnp.float32)
    up_val = jnp.dot(rows, up_part, preferred_element_type=jnp.float32)
    inner = (jax.nn.silu(gate_val) * up_val).astype(jnp.bfloat16)
    return jnp.dot(inner, down_part, preferred_element_type=jnp.float32).astype(jnp.bfloat16)


def reference(cache, cache_scale, lengths, assign, queries, new_kv, hidden, expert_ids, expert_weights, gate_w, up_w, down_w):
    contexts = []
    for group in range(2):
        source = 1 - group
        slot_row = assign[source].astype(jnp.int32)
        slot_cache = jnp.zeros_like(cache[source]).at[slot_row].set(cache[source])
        slot_scale = jnp.zeros_like(cache_scale[source]).at[slot_row].set(cache_scale[source])
        slot_length = jnp.zeros((SLOTS,), jnp.int32).at[slot_row].set(lengths[source].astype(jnp.int32))
        contexts.append(lax.map(attend_slot, (queries[group], new_kv[group], slot_cache, slot_scale, slot_length)))
    context = jnp.stack(contexts)

    tokens = hidden.reshape(-1, D)
    count = tokens.shape[0]
    pair_expert = expert_ids.reshape(-1).astype(jnp.int32)
    pair_weight = expert_weights.reshape(-1).astype(jnp.float32)
    pair_token = (jnp.arange(pair_expert.shape[0], dtype=jnp.int32) // TOP).astype(jnp.int32)
    bound = 2 * N_EP * CAP

    def visit(carry, index):
        hit = pair_expert == index
        slot_rank = jnp.cumsum(hit.astype(jnp.int32)) - 1
        target = jnp.where(hit, slot_rank, bound).astype(jnp.int32)
        buffer = jnp.zeros((bound, D), tokens.dtype).at[target].set(tokens[pair_token], mode="drop")
        produced = expert_apply(buffer, gate_w[index], up_w[index], down_w[index])
        picked = produced[jnp.minimum(target, bound - 1)].astype(jnp.float32)
        picked = picked * jnp.where(hit, pair_weight, jnp.zeros_like(pair_weight))[:, None]
        return carry.at[pair_token].add(picked), None

    mixed, _ = lax.scan(visit, jnp.zeros((count, D), jnp.float32), jnp.arange(EXPERTS, dtype=jnp.int32))
    moe_out = mixed.astype(jnp.bfloat16).reshape(2, SLOTS, STEPS, D)
    return (context, moe_out)
```

```python
import jax
import jax.numpy as jnp
from jax import lax
from jax.sharding import Mesh, PartitionSpec as P

STEPS = 4
LAT = 512
ROPE = 64
QB = 128
D = 3584
TOP = 8
CAP = 2

Y, XH, Z, CORE = 4, 2, 8, 2
PLANE = Y * XH
LINE = Z * CORE
KEEP = LINE * CAP

SCORE_SCALE = 192.0 ** (-0.5)
NEGATIVE = -1e30

LINE_AXES = ("z", "core")
PLANE_AXES = ("y", "xh")
CROSS_AXES = ("pool", "y", "xh")
EP_AXES = ("y", "xh", "z", "core")


def narrowed(value):
    return lax.reduce_precision(value, 8, 7)


def pieces(value):
    first = narrowed(value)
    rest = value - first
    second = narrowed(rest)
    return [part.astype(jnp.bfloat16) for part in (first, second, rest - second)]


def exact_rows(choose, rows):
    return jnp.dot(choose, rows, preferred_element_type=jnp.float32).astype(jnp.bfloat16)


def attend(latent_rows, rope_rows, scale_rows, lengths, query_rows, fresh_keys):
    slot_dev, positions = latent_rows.shape[:2]
    head_count = query_rows.shape[2]
    blocks = LAT // QB
    query_latent = query_rows[..., :LAT].reshape(slot_dev, STEPS, head_count, blocks, QB)
    value_latent = latent_rows.reshape(slot_dev, positions, blocks, QB)
    scale_full = scale_rows.astype(jnp.float32)
    partial_value = jnp.einsum(
        "bshnc,bpnc->bshpn", query_latent, value_latent, preferred_element_type=jnp.float32
    )
    score_cache = jnp.sum(partial_value * scale_full[:, None, None, :, :], axis=-1)
    score_cache = score_cache + jnp.einsum(
        "bshr,bpr->bshp", query_rows[..., LAT:], rope_rows, preferred_element_type=jnp.float32
    )
    score_cache = score_cache * SCORE_SCALE
    position = jnp.arange(positions, dtype=jnp.int32)
    score_cache = jnp.where(
        position[None, None, None, :] < lengths[:, None, None, None], score_cache, NEGATIVE
    )
    score_fresh = (
        jnp.einsum("bshc,btc->bsht", query_rows, fresh_keys, preferred_element_type=jnp.float32)
        * SCORE_SCALE
    )
    step_index = jnp.arange(STEPS, dtype=jnp.int32)
    allowed = step_index[None, None, :] <= step_index[:, None, None]
    score_fresh = jnp.where(allowed[None], score_fresh, NEGATIVE)
    row_max = jnp.maximum(jnp.max(score_cache, axis=-1), jnp.max(score_fresh, axis=-1))[..., None]
    exp_cache = jnp.exp(score_cache - row_max)
    exp_fresh = jnp.exp(score_fresh - row_max)
    summed = jnp.sum(exp_cache, axis=-1, keepdims=True) + jnp.sum(exp_fresh, axis=-1, keepdims=True)
    weight_cache = ((exp_cache / summed)[..., None] * scale_full[:, None, None, :, :]).astype(
        jnp.bfloat16
    )
    weight_fresh = (exp_fresh / summed).astype(jnp.bfloat16)
    latent = jnp.einsum(
        "bshpn,bpnc->bshnc", weight_cache, value_latent, preferred_element_type=jnp.float32
    )
    latent = latent.reshape(slot_dev, STEPS, head_count, LAT)
    latent = latent + jnp.einsum(
        "bsht,btc->bshc", weight_fresh, fresh_keys[..., :LAT], preferred_element_type=jnp.float32
    )
    return latent.astype(jnp.bfloat16)[None]


def on_device(
    cache,
    cache_scale,
    lengths,
    assign,
    queries,
    new_kv,
    hidden,
    expert_ids,
    expert_weights,
    gate_w,
    up_w,
    down_w,
):
    group_self = lax.axis_index("pool")
    yx_self = lax.axis_index(PLANE_AXES)
    zc_self = lax.axis_index(LINE_AXES)
    slot_dev = queries.shape[1]
    slots = assign.shape[1]
    token_count = slot_dev * STEPS
    line_tokens = LINE * token_count

    ids = expert_ids[0].reshape(token_count, TOP).astype(jnp.bfloat16)
    weights = expert_weights[0].reshape(token_count, TOP)
    routing = jnp.concatenate([ids] + pieces(weights), axis=1)
    routing = jnp.pad(routing, ((0, 0), (0, 128 - 4 * TOP)))
    token_rows = jnp.concatenate([hidden[0].reshape(token_count, D), routing], axis=1)
    line = lax.all_gather(token_rows, LINE_AXES, axis=0, tiled=True)

    row_self = lax.dynamic_index_in_dim(assign, group_self, 0, keepdims=False)
    place = jnp.arange(slots, dtype=jnp.int32)
    slot_at = (place // slot_dev % PLANE) * (LINE * slot_dev) + (
        place // (slot_dev * PLANE)
    ) * slot_dev + place % slot_dev
    by_slot = (row_self[None, :] == slot_at[:, None]).astype(jnp.bfloat16)
    stored = jnp.concatenate([cache[0, :, 0, :], cache_scale[0, :, 0, :]], axis=1)
    stored = jnp.pad(stored, ((0, 0), (0, 640 - stored.shape[1])))
    outbound = lax.ppermute(exact_rows(by_slot, stored), "pool", [(0, 1), (1, 0)])
    along = lax.all_to_all(
        outbound.reshape(LINE, PLANE * slot_dev, 640), LINE_AXES, 0, 0, tiled=True
    ).reshape(slots, 640)
    wanted = (place % LINE) * (PLANE * slot_dev) + (
        place // (LINE * slot_dev)
    ) * slot_dev + place // LINE % slot_dev
    shuffle = (place[None, :] == wanted[:, None]).astype(jnp.bfloat16)
    across = lax.all_to_all(
        exact_rows(shuffle, along).reshape(PLANE, slot_dev * LINE, 640), PLANE_AXES, 0, 0, tiled=True
    ).reshape(PLANE, slot_dev, LINE, 640)
    slot_rows = jnp.swapaxes(across, 0, 1).reshape(slot_dev, PLANE * LINE, 640)

    length_other = lax.dynamic_index_in_dim(lengths, 1 - group_self, 0, keepdims=False)
    row_other = lax.dynamic_index_in_dim(assign, 1 - group_self, 0, keepdims=False)
    my_slots = (yx_self * LINE + zc_self) * slot_dev + jnp.arange(slot_dev, dtype=jnp.int32)
    my_length = jnp.sum(
        jnp.where(row_other[None, :] == my_slots[:, None], length_other[None, :], 0), axis=1
    )

    line_ids = line[:, D : D + TOP].astype(jnp.int32)
    line_weights = sum(
        line[:, D + TOP * part : D + TOP * (part + 1)].astype(jnp.float32) for part in (1, 2, 3)
    )
    experts = jnp.arange(PLANE, dtype=jnp.int32) * LINE + zc_self
    named = line_ids[None, :, :] == experts[:, None, None]
    hit = jnp.any(named, axis=2)
    weight_of = jnp.sum(jnp.where(named, line_weights[None], 0.0), axis=2)
    earlier = (
        jnp.arange(line_tokens)[:, None] < jnp.arange(line_tokens)[None, :]
    ).astype(jnp.bfloat16)
    rank = jnp.dot(
        hit.astype(jnp.bfloat16), earlier, preferred_element_type=jnp.float32
    ).astype(jnp.int32)
    rank = jnp.where(hit, rank, -1)
    chosen = rank[:, None, :] == jnp.arange(KEEP, dtype=jnp.int32)[None, :, None]
    choose = chosen.astype(jnp.bfloat16).reshape(PLANE * KEEP, line_tokens)
    rows = exact_rows(choose, line[:, :D])
    sent = jnp.concatenate([rows, rows], axis=0).reshape(2 * PLANE, KEEP, D)
    taken = lax.all_to_all(sent, CROSS_AXES, 0, 0, tiled=True).reshape(2 * PLANE * KEEP, D)

    gate_val = jnp.dot(taken, gate_w[0], preferred_element_type=jnp.float32)
    up_val = jnp.dot(taken, up_w[0], preferred_element_type=jnp.float32)
    inner = (jax.nn.silu(gate_val) * up_val).astype(jnp.bfloat16)
    served = jnp.dot(inner, down_w[0], preferred_element_type=jnp.float32).astype(jnp.bfloat16)
    back = lax.all_to_all(
        served.reshape(2 * PLANE, KEEP, D), CROSS_AXES, 0, 0, tiled=True
    ).reshape(2 * PLANE * KEEP, D)

    mix = jnp.where(chosen, weight_of[:, None, :], 0.0).reshape(PLANE * KEEP, line_tokens).T
    mix_high = narrowed(mix)
    mix_parts = [part.astype(jnp.bfloat16) for part in (mix_high, mix - mix_high)]
    mixed = sum(
        jnp.dot(jnp.concatenate([part, part], axis=1), back, preferred_element_type=jnp.float32)
        for part in mix_parts
    ).astype(jnp.bfloat16)
    gathered = lax.all_to_all(
        mixed.reshape(LINE, token_count, D), LINE_AXES, 0, 0, tiled=True
    )
    moe_out = jnp.sum(gathered.astype(jnp.float32), axis=0).astype(jnp.bfloat16)

    context = attend(
        slot_rows[..., :LAT],
        slot_rows[..., LAT : LAT + ROPE],
        slot_rows[..., LAT + ROPE : LAT + ROPE + LAT // QB],
        my_length,
        queries[0],
        new_kv[0],
    )
    return (context, moe_out.reshape(1, slot_dev, STEPS, D))


def solution(mesh):
    fine = Mesh(
        mesh.devices.reshape(2, Y, XH, Z, CORE), ("pool", "y", "xh", "z", "core")
    )
    return jax.shard_map(
        on_device,
        mesh=fine,
        in_specs=(
            P("pool", None, EP_AXES, None),
            P("pool", None, EP_AXES, None),
            P(),
            P(),
            P("pool", EP_AXES, None, None, None),
            P("pool", EP_AXES, None, None),
            P("pool", EP_AXES, None, None),
            P("pool", EP_AXES, None, None),
            P("pool", EP_AXES, None, None),
            P(EP_AXES, None, "pool"),
            P(EP_AXES, None, "pool"),
            P(EP_AXES, "pool", None),
        ),
        out_specs=(P("pool", EP_AXES, None, None, None), P("pool", EP_AXES, None, None)),
        check_vma=False,
    )
```

```python
import jax
import jax.numpy as jnp
from jax import lax
from jax.experimental import pallas as pl
from jax.experimental.pallas import tpu as pltpu
from jax.sharding import Mesh, PartitionSpec as P

STEPS = 4
LAT = 512
ROPE = 64
QB = 128
D = 3584
TOP = 8
CAP = 2

Y, XH, Z, CORE = 4, 2, 8, 2
PLANE = Y * XH
LINE = Z * CORE
KEEP = LINE * CAP
ROW = 640
SIDE = 384

SCORE_SCALE = 192.0 ** (-0.5)
NEGATIVE = -1e30

LINE_AXES = ("z", "core")
PLANE_AXES = ("y", "xh")
CROSS_AXES = ("pool", "y", "xh")
EP_AXES = ("y", "xh", "z", "core")


WIDE = D + 128
BLOCK = 512
MIB = 1 << 20


def dispatch_kernel(own_ref, line_ref, kept_ref, given_ref, sent_ref, mix_ref):
    group, zc = own_ref[0], own_ref[1]
    tokens = line_ref.shape[0]
    routing = line_ref[:, D:].astype(jnp.float32).T
    token = lax.broadcasted_iota(jnp.int32, (tokens, tokens), 0)
    other = lax.broadcasted_iota(jnp.int32, (tokens, tokens), 1)
    ids = routing[:TOP].astype(jnp.int32)
    weights = routing[TOP : 2 * TOP] + routing[2 * TOP : 3 * TOP] + routing[3 * TOP : 4 * TOP]
    hits, shares = [], []
    for place in range(PLANE):
        named = ids == place * LINE + zc
        hits.append(jnp.sum(jnp.where(named, 1.0, 0.0), axis=0, keepdims=True))
        shares.append(jnp.sum(jnp.where(named, weights, 0.0), axis=0, keepdims=True))
    hit = jnp.concatenate(hits, axis=0)
    rank = jnp.dot(
        hit.astype(jnp.bfloat16),
        jnp.where(token < other, 1.0, 0.0).astype(jnp.bfloat16),
        preferred_element_type=jnp.float32,
    )
    rank = jnp.where(hit > 0.0, rank, -1.0).astype(jnp.int32)
    seat = lax.broadcasted_iota(jnp.int32, (KEEP, tokens), 0)
    chosen = [seat == rank[place : place + 1] for place in range(PLANE)]
    choose = jnp.concatenate([jnp.where(c, 1.0, 0.0) for c in chosen], axis=0)
    choose = choose.astype(jnp.bfloat16)
    group_of = Z * tokens // LINE
    device = tokens // LINE
    source = (other % group_of) // device * (CORE * device) + other // group_of * device
    source = source + other % device
    regroup = jnp.where(token == source, 1.0, 0.0).astype(jnp.bfloat16)
    mix = jnp.concatenate(
        [jnp.where(chosen[place], shares[place], 0.0) for place in range(PLANE)], axis=0
    )
    high = mix.astype(jnp.bfloat16)
    low = (mix - high.astype(jnp.float32)).astype(jnp.bfloat16)
    for index, part in enumerate((high, low)):
        turned_part = lax.dot_general(
            regroup, part, (((0,), (1,)), ((), ())), preferred_element_type=jnp.float32
        ).astype(jnp.bfloat16)
        mix_ref[index] = jnp.concatenate([turned_part, turned_part], axis=1)
    count = PLANE * KEEP
    for start in range(0, D, BLOCK):
        columns = pl.ds(start, BLOCK)
        rows = jnp.dot(choose, line_ref[:, columns], preferred_element_type=jnp.float32)
        rows = rows.astype(jnp.bfloat16)
        sent_ref[pl.ds(0, count), columns] = rows
        sent_ref[pl.ds(count, count), columns] = rows
    for half, ref in ((group, given_ref), (1 - group, kept_ref)):
        for place in range(PLANE):
            top = pl.multiple_of(half * count + place * KEEP, KEEP)
            rows = ref[pl.ds(place * LINE, LINE), :]
            sent_ref[pl.ds(top, LINE), pl.ds(D, SIDE)] = rows[:, :SIDE]
            tail = jnp.concatenate(
                [rows[:, SIDE:], jnp.zeros((LINE, 2 * SIDE - ROW), jnp.bfloat16)], axis=1
            )
            sent_ref[pl.ds(top + LINE, LINE), pl.ds(D, SIDE)] = tail


def dispatch(own, line, kept, given):
    tokens = line.shape[0]
    count = 2 * PLANE * KEEP
    vmem = pl.BlockSpec(memory_space=pltpu.VMEM)
    return pl.pallas_call(
        dispatch_kernel,
        out_shape=(
            jax.ShapeDtypeStruct((count, D + SIDE), jnp.bfloat16),
            jax.ShapeDtypeStruct((2, tokens, count), jnp.bfloat16),
        ),
        in_specs=[pl.BlockSpec(memory_space=pltpu.SMEM), vmem, vmem, vmem],
        out_specs=(vmem, vmem),
        compiler_params=pltpu.CompilerParams(vmem_limit_bytes=24 * MIB),
        name="dispatch",
    )(own, line, kept, given)


def turn_kernel(one_ref, two_ref, three_ref, out_ref):
    rows = out_ref.shape[0]
    slot_dev = out_ref.shape[1] // ROW
    to = lax.broadcasted_iota(jnp.int32, (rows, rows), 0)
    at = lax.broadcasted_iota(jnp.int32, (rows, rows), 1)
    core, z, yx = to // (Z * PLANE), to // PLANE % Z, to % PLANE
    turn = jnp.where(at == yx * LINE + z * CORE + core, 1.0, 0.0).astype(jnp.bfloat16)
    for b in range(slot_dev):
        heads, tails = [], []
        for place in range(b * PLANE, (b + 1) * PLANE):
            first = pl.ds(place * KEEP, LINE)
            second = pl.ds(place * KEEP + LINE, LINE)
            heads.append(
                jnp.concatenate([r[first, :] for r in (one_ref, two_ref, three_ref)], axis=1)
            )
            tails.append(jnp.concatenate([r[second, :] for r in (one_ref, two_ref)], axis=1))
        for parts, start in ((heads, 0), (tails, SIDE)):
            part = jnp.concatenate(parts, axis=0)
            moved = jnp.dot(turn, part, preferred_element_type=jnp.float32).astype(jnp.bfloat16)
            out_ref[:, pl.ds(b * ROW + start, part.shape[1])] = moved


def turned(taken, slot_dev):
    rows = taken.shape[0]
    shape = (PLANE * LINE, slot_dev * ROW)
    return pl.pallas_call(
        turn_kernel,
        grid=(1,),
        out_shape=jax.ShapeDtypeStruct(shape, jnp.bfloat16),
        in_specs=[
            pl.BlockSpec((rows, 128), lambda i, at=at: (0, D // 128 + at)) for at in range(3)
        ],
        out_specs=pl.BlockSpec(shape, lambda i: (0, 0)),
        compiler_params=pltpu.CompilerParams(vmem_limit_bytes=12 * MIB),
        name="turned",
    )(taken, taken, taken)


def expert_kernel(taken_ref, gate_ref, up_ref, down_ref, out_ref, inner, down, done):
    copy = pltpu.make_async_copy(down_ref, down, done)
    copy.start()
    width = inner.shape[1]
    for start in range(0, width, 256):
        columns = pl.ds(start, 256)
        rows = taken_ref[:, pl.ds(0, D)]
        gate = jnp.dot(rows, gate_ref[:, columns], preferred_element_type=jnp.float32)
        up = jnp.dot(rows, up_ref[:, columns], preferred_element_type=jnp.float32)
        inner[:, columns] = (jax.nn.silu(gate) * up).astype(jnp.bfloat16)
    copy.wait()
    for start in range(0, D, BLOCK):
        columns = pl.ds(start, BLOCK)
        out_ref[:, columns] = jnp.dot(
            inner[...], down[:, columns], preferred_element_type=jnp.float32
        ).astype(jnp.bfloat16)


def expert(taken, gate, up, down):
    count, width = taken.shape[0], gate.shape[1]
    vmem = pl.BlockSpec(memory_space=pltpu.VMEM)
    return pl.pallas_call(
        expert_kernel,
        out_shape=jax.ShapeDtypeStruct((count, D), jnp.bfloat16),
        in_specs=[vmem, vmem, vmem, pl.BlockSpec(memory_space=pl.ANY)],
        out_specs=vmem,
        scratch_shapes=[
            pltpu.VMEM((count, width), jnp.bfloat16),
            pltpu.VMEM((width, D), jnp.bfloat16),
            pltpu.SemaphoreType.DMA,
        ],
        compiler_params=pltpu.CompilerParams(vmem_limit_bytes=28 * MIB),
        cost_estimate=pl.CostEstimate(
            flops=6 * count * width * D, bytes_accessed=6 * width * D + 4 * count * D, transcendentals=0
        ),
        name="expert",
    )(taken, gate, up, down)


def combine_kernel(mix_ref, back_ref, beside_ref, out_ref):
    for start in range(0, D, BLOCK):
        columns = pl.ds(start, BLOCK)
        back = back_ref[:, columns]
        total = jnp.dot(mix_ref[0], back, preferred_element_type=jnp.float32)
        total = total + jnp.dot(mix_ref[1], back, preferred_element_type=jnp.float32)
        out_ref[:, columns] = total.astype(jnp.bfloat16)
    out_ref[:, pl.ds(D, beside_ref.shape[1])] = beside_ref[...]


def combine(mix, back, beside):
    vmem = pl.BlockSpec(memory_space=pltpu.VMEM)
    return pl.pallas_call(
        combine_kernel,
        out_shape=jax.ShapeDtypeStruct((mix.shape[1], D + beside.shape[1]), jnp.bfloat16),
        in_specs=[vmem, vmem, vmem],
        out_specs=vmem,
        compiler_params=pltpu.CompilerParams(vmem_limit_bytes=12 * MIB),
        name="combine",
    )(mix, back, beside)


def pair_kernel(pair_ref, out_ref):
    total = pair_ref[0, :, pl.ds(0, D)].astype(jnp.float32)
    for core in range(1, CORE):
        total = total + pair_ref[core, :, pl.ds(0, D)].astype(jnp.float32)
    out_ref[:, pl.ds(0, D)] = total.astype(jnp.bfloat16)
    beside = pair_ref.shape[2] - D
    for core in range(CORE):
        out_ref[:, pl.ds(D + core * beside, beside)] = pair_ref[core, :, pl.ds(D, beside)]


def paired(pair):
    cores, rows, width = pair.shape
    vmem = pl.BlockSpec(memory_space=pltpu.VMEM)
    return pl.pallas_call(
        pair_kernel,
        out_shape=jax.ShapeDtypeStruct((rows, D + cores * (width - D)), jnp.bfloat16),
        in_specs=[vmem],
        out_specs=vmem,
        compiler_params=pltpu.CompilerParams(vmem_limit_bytes=12 * MIB),
        name="paired",
    )(pair)


def prepare_kernel(
    own_ref, assign_ref, cache_ref, scale_ref, hidden_ref, ids_ref, weights_ref,
    kept_ref, given_ref, tokens_ref,
):
    group = own_ref[0]
    slot_dev = hidden_ref.shape[0]
    half_slots = kept_ref.shape[0]
    requests = assign_ref.shape[1]
    hidden = [hidden_ref[b].astype(jnp.float32) for b in range(slot_dev)]
    tokens_ref[:, pl.ds(0, D)] = jnp.concatenate(hidden, axis=0).astype(jnp.bfloat16)
    ids = jnp.concatenate([ids_ref[b].astype(jnp.float32) for b in range(slot_dev)], axis=0)
    rest = jnp.concatenate([weights_ref[b] for b in range(slot_dev)], axis=0)
    terms = [ids.astype(jnp.bfloat16)]
    for _ in range(3):
        term = rest.astype(jnp.bfloat16)
        rest = rest - term.astype(jnp.float32)
        terms.append(term)
    at = lax.broadcasted_iota(jnp.int32, (TOP, WIDE - D), 0)
    lane = lax.broadcasted_iota(jnp.int32, (TOP, WIDE - D), 1)
    routing = sum(
        jnp.dot(
            term,
            jnp.where(lane == at + TOP * index, 1.0, 0.0).astype(jnp.bfloat16),
            preferred_element_type=jnp.float32,
        )
        for index, term in enumerate(terms)
    )
    tokens_ref[:, pl.ds(D, WIDE - D)] = routing.astype(jnp.bfloat16)
    row = jnp.where(group == 0, assign_ref[0:1, :], assign_ref[1:2, :])
    tail = jnp.concatenate(
        [
            scale_ref[...].astype(jnp.float32),
            jnp.zeros((ROW - LAT - ROPE - LAT // QB, requests), jnp.float32),
        ],
        axis=0,
    ).astype(jnp.bfloat16)
    stored = jnp.concatenate([cache_ref[...], tail], axis=0)
    place = lax.broadcasted_iota(jnp.int32, (half_slots, requests), 0) * slot_dev
    for half, ref in ((group, kept_ref), (1 - group, given_ref)):
        choose = jnp.where(place + half == row, 1.0, 0.0).astype(jnp.bfloat16)
        ref[...] = lax.dot_general(
            choose, stored, (((1,), (1,)), ((), ())), preferred_element_type=jnp.float32
        ).astype(jnp.bfloat16)


def prepare(own, assign, cache, scale, hidden, ids, weights):
    half_slots = assign.shape[1] // hidden.shape[0]
    tokens = hidden.shape[0] * STEPS
    args = (own, assign, cache, scale, hidden, ids, weights)
    shapes = ((half_slots, ROW), (half_slots, ROW), (tokens, WIDE))

    def whole(shape):
        return pl.BlockSpec(shape, lambda i: (0,) * len(shape))

    return pl.pallas_call(
        prepare_kernel,
        grid=(1,),
        out_shape=[jax.ShapeDtypeStruct(shape, jnp.bfloat16) for shape in shapes],
        in_specs=[pl.BlockSpec(memory_space=pltpu.SMEM)] + [whole(a.shape) for a in args[1:]],
        out_specs=[whole(shape) for shape in shapes],
        compiler_params=pltpu.CompilerParams(vmem_limit_bytes=58 * MIB),
        name="prepare",
    )(*args)


def finish_kernel(
    own_ref, assign_ref, lengths_ref, gathered_ref, query_ref, fresh_ref, out_ref, moe_ref
):
    group, zc, yx = own_ref[0], own_ref[1], own_ref[2]
    slot_dev, rows = query_ref.shape[:2]
    lines, width = gathered_ref.shape
    positions = CORE * lines
    blocks = LAT // QB
    device = slot_dev * STEPS
    total = sum(
        gathered_ref[pl.ds(z * device, device), pl.ds(0, D)].astype(jnp.float32) for z in range(Z)
    ).astype(jnp.bfloat16)
    for b in range(slot_dev):
        moe_ref[b] = total[b * STEPS : (b + 1) * STEPS]
    assigned = jnp.where(group == 0, assign_ref[1:2, :], assign_ref[0:1, :])
    lengths = jnp.where(group == 0, lengths_ref[1:2, :], lengths_ref[0:1, :])
    lane = lax.broadcasted_iota(jnp.int32, (rows, positions), 1)
    position = lane % PLANE * LINE + lane // PLANE % Z * CORE + lane // lines
    new = 16
    step = lax.broadcasted_iota(jnp.int32, (rows, new), 0) // (rows // STEPS)
    token = lax.broadcasted_iota(jnp.int32, (rows, new), 1)
    by_rows = (((1,), (1,)), ((), ()))
    for b in range(slot_dev):
        slot = (yx * LINE + zc) * slot_dev + b
        length = jnp.sum(jnp.where(assigned == slot, lengths, 0), axis=1, keepdims=True)
        keys = jnp.concatenate(
            [
                gathered_ref[:, pl.ds(D + (core * slot_dev + b) * ROW, ROW)]
                for core in range(CORE)
            ],
            axis=0,
        )
        scale = keys[:, LAT:].astype(jnp.float32).T[ROPE : ROPE + blocks]
        score = lax.dot_general(
            query_ref[b, :, pl.ds(LAT, ROPE)],
            keys[:, LAT : LAT + ROPE],
            by_rows,
            preferred_element_type=jnp.float32,
        )
        for n in range(blocks):
            part = lax.dot_general(
                query_ref[b, :, pl.ds(n * QB, QB)],
                keys[:, n * QB : (n + 1) * QB],
                by_rows,
                preferred_element_type=jnp.float32,
            )
            score = score + part * scale[n : n + 1]
        score = jnp.where(position < length, score * SCORE_SCALE, NEGATIVE)
        fresh = jnp.concatenate(
            [fresh_ref[b].astype(jnp.float32), jnp.zeros((new - STEPS, LAT + ROPE), jnp.float32)],
            axis=0,
        ).astype(jnp.bfloat16)
        score_fresh = lax.dot_general(
            query_ref[b], fresh, by_rows, preferred_element_type=jnp.float32
        )
        score_fresh = jnp.where(token <= step, score_fresh * SCORE_SCALE, NEGATIVE)
        top = jnp.maximum(
            jnp.max(score, axis=1, keepdims=True), jnp.max(score_fresh, axis=1, keepdims=True)
        )
        exp_cache, exp_fresh = jnp.exp(score - top), jnp.exp(score_fresh - top)
        summed = jnp.sum(exp_cache, axis=1, keepdims=True)
        summed = summed + jnp.sum(exp_fresh, axis=1, keepdims=True)
        prob = exp_cache / summed
        weight_fresh = (exp_fresh / summed).astype(jnp.bfloat16)
        for n in range(blocks):
            columns = slice(n * QB, (n + 1) * QB)
            weight = (prob * scale[n : n + 1]).astype(jnp.bfloat16)
            latent = jnp.dot(weight, keys[:, columns], preferred_element_type=jnp.float32)
            latent = latent + jnp.dot(
                weight_fresh, fresh[:, columns], preferred_element_type=jnp.float32
            )
            out_ref[b, :, pl.ds(n * QB, QB)] = latent.astype(jnp.bfloat16)


def finish(own, assign, lengths, gathered, queries, fresh):
    slot_dev, rows = queries.shape[:2]
    vmem = pl.BlockSpec(memory_space=pltpu.VMEM)
    return pl.pallas_call(
        finish_kernel,
        out_shape=(
            jax.ShapeDtypeStruct((slot_dev, rows, LAT), jnp.bfloat16),
            jax.ShapeDtypeStruct((slot_dev, STEPS, D), jnp.bfloat16),
        ),
        in_specs=[pl.BlockSpec(memory_space=pltpu.SMEM)] + [vmem] * 5,
        out_specs=(vmem, vmem),
        compiler_params=pltpu.CompilerParams(vmem_limit_bytes=16 * MIB),
        name="finish",
    )(own, assign, lengths, gathered, queries, fresh)


def on_device(
    cache,
    cache_scale,
    lengths,
    assign,
    queries,
    new_kv,
    hidden,
    expert_ids,
    expert_weights,
    gate_w,
    up_w,
    down_w,
):
    slot_dev, heads = queries.shape[1], queries.shape[3]
    token_count = slot_dev * STEPS
    own = jnp.stack(
        [lax.axis_index("pool"), lax.axis_index(LINE_AXES), lax.axis_index(PLANE_AXES)]
    ).astype(jnp.int32)
    kept, given, token_rows = prepare(
        own,
        assign,
        cache[0, :, 0, :].T,
        cache_scale[0, :, 0, :].T,
        hidden[0],
        expert_ids[0],
        expert_weights[0],
    )
    given = lax.ppermute(given, "pool", [(0, 1), (1, 0)])
    line = lax.all_gather(token_rows, LINE_AXES, axis=0, tiled=True)
    line, given = lax.optimization_barrier((line, given))

    sent, mix = dispatch(own, line, kept, given)
    taken = lax.all_to_all(
        sent.reshape(2 * PLANE, KEEP, D + SIDE), CROSS_AXES, 0, 0, tiled=True
    ).reshape(2 * PLANE * KEEP, D + SIDE)

    served = expert(taken, gate_w[0], up_w[0], down_w[0])

    beside = turned(taken, slot_dev)
    served, beside = lax.optimization_barrier((served, beside))
    back = lax.all_to_all(
        served.reshape(2 * PLANE, KEEP, D), CROSS_AXES, 0, 0, tiled=True
    ).reshape(2 * PLANE * KEEP, D)

    mixed = combine(mix, back, beside).reshape(CORE, Z * token_count, -1)
    pair = paired(lax.all_to_all(mixed, "core", 0, 0, tiled=True))
    gathered = lax.all_to_all(pair.reshape(Z, token_count, -1), "z", 0, 0, tiled=True)
    context, moe_out = finish(
        own,
        assign,
        lengths,
        gathered.reshape(pair.shape),
        queries[0].reshape(slot_dev, STEPS * heads, -1),
        new_kv[0],
    )
    return (
        context.reshape(1, slot_dev, STEPS, heads, LAT),
        moe_out.reshape(1, slot_dev, STEPS, D),
    )


def solution(mesh):
    fine = Mesh(
        mesh.devices.reshape(2, Y, XH, Z, CORE), ("pool", "y", "xh", "z", "core")
    )
    return jax.shard_map(
        on_device,
        mesh=fine,
        in_specs=(
            P("pool", None, EP_AXES, None),
            P("pool", None, EP_AXES, None),
            P(),
            P(),
            P("pool", EP_AXES, None, None, None),
            P("pool", EP_AXES, None, None),
            P("pool", EP_AXES, None, None),
            P("pool", EP_AXES, None, None),
            P("pool", EP_AXES, None, None),
            P(EP_AXES, None, "pool"),
            P(EP_AXES, None, "pool"),
            P(EP_AXES, "pool", None),
        ),
        out_specs=(P("pool", EP_AXES, None, None, None), P("pool", EP_AXES, None, None)),
        check_vma=False,
    )
```

```python
import jax
import jax.numpy as jnp
from jax import lax
from jax.experimental import pallas as pl
from jax.experimental.pallas import tpu as pltpu
from jax.sharding import Mesh, PartitionSpec as P

STEPS = 4
LAT = 512
ROPE = 64
QB = 128
D = 3584
TOP = 8
CAP = 2

Y, XH, LINE, ZL, CORE = 4, 2, 4, 2, 2
FOUR = ZL * CORE
PLANE = Y * XH * FOUR
KEEP = LINE * CAP
ROW = 640
SIDE = 384
SPREAD = 8

SCORE_SCALE = 192.0 ** (-0.5)
NEGATIVE = -1e30

LINE_AXES = "zh"
CROSS_AXES = ("pool", "y", "xh", "zl", "core")
EP_AXES = ("y", "xh", "zh", "zl", "core")


WIDE = D + 128
BLOCK = 512
MIB = 1 << 20


def whole(shape):
    return pl.BlockSpec(shape, lambda i: (0,) * len(shape))


def dispatch_kernel(line_ref, kept_ref, given_ref, sent_ref, mix_ref):
    group, zh = lax.axis_index("pool"), lax.axis_index(LINE_AXES)
    tokens = line_ref.shape[0]
    routing = jnp.concatenate(
        [line_ref[:, pl.ds(D, 128)].astype(jnp.float32), jnp.zeros((128 - tokens, 128), jnp.float32)],
        axis=0,
    ).T[:, :tokens]
    place = lax.broadcasted_iota(jnp.int32, (PLANE, tokens), 0)
    expert_at = place // FOUR * (LINE * FOUR) + zh * FOUR + place % FOUR
    hit = jnp.zeros((PLANE, tokens), jnp.float32)
    share = jnp.zeros((PLANE, tokens), jnp.float32)
    for k in range(TOP):
        weight = sum(routing[TOP * part + k : TOP * part + k + 1] for part in (1, 2, 3))
        named = routing[k : k + 1].astype(jnp.int32) == expert_at
        hit = hit + jnp.where(named, 1.0, 0.0)
        share = share + jnp.where(named, weight, 0.0)
    token = lax.broadcasted_iota(jnp.int32, (tokens, tokens), 0)
    other = lax.broadcasted_iota(jnp.int32, (tokens, tokens), 1)
    rank = jnp.dot(
        hit.astype(jnp.bfloat16),
        jnp.where(token < other, 1.0, 0.0).astype(jnp.bfloat16),
        preferred_element_type=jnp.float32,
    )
    rank = jnp.where(hit > 0.0, rank, -1.0).astype(jnp.int32)
    seat = lax.broadcasted_iota(jnp.int32, (KEEP, tokens), 0)
    chosen = [seat == rank[e : e + 1] for e in range(PLANE)]
    choose = jnp.concatenate([jnp.where(c, 1.0, 0.0) for c in chosen], axis=0)
    choose = choose.astype(jnp.bfloat16)
    mix = jnp.concatenate(
        [jnp.where(chosen[e], share[e : e + 1], 0.0) for e in range(PLANE)], axis=0
    )
    high = mix.astype(jnp.bfloat16)
    low = (mix - high.astype(jnp.float32)).astype(jnp.bfloat16)
    same = jnp.where(token == other, 1.0, 0.0).astype(jnp.bfloat16)
    for index, part in enumerate((high, low)):
        across = lax.dot_general(
            same, part, (((1,), (1,)), ((), ())), preferred_element_type=jnp.float32
        ).astype(jnp.bfloat16)
        mix_ref[index] = jnp.concatenate([across, across], axis=1)
    count = PLANE * KEEP
    for start in range(0, D, BLOCK):
        columns = pl.ds(start, BLOCK)
        rows = jnp.dot(choose, line_ref[:, columns], preferred_element_type=jnp.float32)
        rows = rows.astype(jnp.bfloat16)
        sent_ref[pl.ds(0, count), columns] = rows
        sent_ref[pl.ds(count, count), columns] = rows
    for half, ref in ((group, given_ref), (1 - group, kept_ref)):
        top = pl.multiple_of(half * count, count)
        sent_ref[pl.ds(top, count), pl.ds(D, SIDE)] = ref[...]


def dispatch(line, kept, given):
    tokens = line.shape[0]
    count = 2 * PLANE * KEEP
    vmem = pl.BlockSpec(memory_space=pltpu.VMEM)
    return pl.pallas_call(
        dispatch_kernel,
        out_shape=(
            jax.ShapeDtypeStruct((count, D + SIDE), jnp.bfloat16),
            jax.ShapeDtypeStruct((2, tokens, count), jnp.bfloat16),
        ),
        in_specs=[vmem, vmem, vmem],
        out_specs=(vmem, vmem),
        compiler_params=pltpu.CompilerParams(vmem_limit_bytes=24 * MIB),
        cost_estimate=pl.CostEstimate(
            flops=2 * count * tokens * D, bytes_accessed=8 * count * D, transcendentals=0
        ),
        name="dispatch",
    )(line, kept, given)


def turn_kernel(one_ref, two_ref, three_ref, out_ref):
    rows = out_ref.shape[0]
    group = SPREAD * KEEP
    to = lax.broadcasted_iota(jnp.int32, (rows, group), 0)
    at = lax.broadcasted_iota(jnp.int32, (rows, group), 1)
    first = to % SPREAD * KEEP + to // SPREAD
    for index in range(out_ref.shape[1] // ROW):
        block = pl.ds(index * group, group)
        three = jnp.concatenate([r[block, :] for r in (one_ref, two_ref, three_ref)], axis=1)
        for part, (start, width) in enumerate(((0, SIDE), (SIDE, ROW - SIDE))):
            turn = jnp.where(at == first + part * LINE, 1.0, 0.0).astype(jnp.bfloat16)
            moved = jnp.dot(turn, three[:, :width], preferred_element_type=jnp.float32)
            out_ref[:, pl.ds(index * ROW + start, width)] = moved.astype(jnp.bfloat16)


def turned(taken):
    rows = taken.shape[0]
    shape = (LINE * SPREAD, rows // (SPREAD * KEEP) * ROW)
    return pl.pallas_call(
        turn_kernel,
        grid=(1,),
        out_shape=jax.ShapeDtypeStruct(shape, jnp.bfloat16),
        in_specs=[
            pl.BlockSpec((rows, 128), lambda i, at=at: (0, D // 128 + at)) for at in range(3)
        ],
        out_specs=whole(shape),
        compiler_params=pltpu.CompilerParams(vmem_limit_bytes=12 * MIB),
        name="turned",
    )(taken, taken, taken)


def expert_kernel(taken_ref, gate_ref, up_ref, down_ref, out_ref, inner, down, done):
    copy = pltpu.make_async_copy(down_ref, down, done)
    copy.start()
    width = inner.shape[1]
    for start in range(0, width, 256):
        columns = pl.ds(start, 256)
        rows = taken_ref[:, pl.ds(0, D)]
        gate = jnp.dot(rows, gate_ref[:, columns], preferred_element_type=jnp.float32)
        up = jnp.dot(rows, up_ref[:, columns], preferred_element_type=jnp.float32)
        inner[:, columns] = (jax.nn.silu(gate) * up).astype(jnp.bfloat16)
    copy.wait()
    for start in range(0, D, BLOCK):
        columns = pl.ds(start, BLOCK)
        out_ref[:, columns] = jnp.dot(
            inner[...], down[:, columns], preferred_element_type=jnp.float32
        ).astype(jnp.bfloat16)


def expert(taken, gate, up, down):
    count, width = taken.shape[0], gate.shape[1]
    vmem = pl.BlockSpec(memory_space=pltpu.VMEM)
    return pl.pallas_call(
        expert_kernel,
        out_shape=jax.ShapeDtypeStruct((count, D), jnp.bfloat16),
        in_specs=[vmem, vmem, vmem, pl.BlockSpec(memory_space=pl.ANY)],
        out_specs=vmem,
        scratch_shapes=[
            pltpu.VMEM((count, width), jnp.bfloat16),
            pltpu.VMEM((width, D), jnp.bfloat16),
            pltpu.SemaphoreType.DMA,
        ],
        compiler_params=pltpu.CompilerParams(vmem_limit_bytes=28 * MIB),
        cost_estimate=pl.CostEstimate(
            flops=6 * count * width * D, bytes_accessed=6 * width * D + 4 * count * D, transcendentals=0
        ),
        name="expert",
    )(taken, gate, up, down)


def combine_kernel(mix_ref, back_ref, beside_ref, out_ref):
    for start in range(0, D, BLOCK):
        columns = pl.ds(start, BLOCK)
        back = back_ref[:, columns]
        total = jnp.dot(mix_ref[0], back, preferred_element_type=jnp.float32)
        total = total + jnp.dot(mix_ref[1], back, preferred_element_type=jnp.float32)
        out_ref[:, columns] = total.astype(jnp.bfloat16)
    out_ref[:, pl.ds(D, beside_ref.shape[1])] = beside_ref[...]


def combine(mix, back, beside):
    vmem = pl.BlockSpec(memory_space=pltpu.VMEM)
    return pl.pallas_call(
        combine_kernel,
        out_shape=jax.ShapeDtypeStruct((mix.shape[1], D + beside.shape[1]), jnp.bfloat16),
        in_specs=[vmem, vmem, vmem],
        out_specs=vmem,
        compiler_params=pltpu.CompilerParams(vmem_limit_bytes=12 * MIB),
        name="combine",
    )(mix, back, beside)


def prepare_kernel(
    assign_ref, cache_ref, scale_ref, hidden_ref, ids_ref, weights_ref,
    kept_ref, given_ref, tokens_ref,
):
    group = lax.axis_index("pool")
    slot_dev = hidden_ref.shape[0]
    requests = assign_ref.shape[1]
    hidden = [hidden_ref[b].astype(jnp.float32) for b in range(slot_dev)]
    hidden = jnp.concatenate(hidden, axis=0)
    ids = jnp.concatenate([ids_ref[b].astype(jnp.float32) for b in range(slot_dev)], axis=0)
    rest = jnp.concatenate([weights_ref[b] for b in range(slot_dev)], axis=0)
    terms = [ids.astype(jnp.bfloat16)]
    for _ in range(3):
        term = rest.astype(jnp.bfloat16)
        rest = rest - term.astype(jnp.float32)
        terms.append(term)
    at = lax.broadcasted_iota(jnp.int32, (TOP, WIDE - D), 0)
    lane = lax.broadcasted_iota(jnp.int32, (TOP, WIDE - D), 1)
    routing = sum(
        jnp.dot(
            term,
            jnp.where(lane == at + TOP * index, 1.0, 0.0).astype(jnp.bfloat16),
            preferred_element_type=jnp.float32,
        )
        for index, term in enumerate(terms)
    )
    row = jnp.concatenate([hidden, routing], axis=1)
    tokens_ref[...] = jnp.concatenate([row] * LINE, axis=0).astype(jnp.bfloat16)
    row = jnp.where(group == 0, assign_ref[0:1, :], assign_ref[1:2, :])
    tail = jnp.concatenate(
        [
            scale_ref[...].astype(jnp.float32),
            jnp.zeros((ROW - LAT - ROPE - LAT // QB, requests), jnp.float32),
        ],
        axis=0,
    ).astype(jnp.bfloat16)
    stored = jnp.concatenate([cache_ref[...], tail], axis=0)
    at = lax.broadcasted_iota(jnp.int32, (PLANE * KEEP, requests), 0)
    place, zh = at // KEEP, at % LINE
    slot = (place // FOUR * (LINE * FOUR) + zh * FOUR + place % FOUR) * slot_dev
    head = lax.broadcasted_iota(jnp.int32, (PLANE * KEEP, SIDE), 0) % KEEP < LINE
    for half, ref in ((group, kept_ref), (1 - group, given_ref)):
        choose = jnp.where(slot + half == row, 1.0, 0.0).astype(jnp.bfloat16)
        found = lax.dot_general(
            choose, stored, (((1,), (1,)), ((), ())), preferred_element_type=jnp.float32
        )
        tail = jnp.concatenate(
            [found[:, SIDE:], jnp.zeros((PLANE * KEEP, 2 * SIDE - ROW), jnp.float32)], axis=1
        )
        ref[...] = jnp.where(head, found[:, :SIDE], tail).astype(jnp.bfloat16)


def prepare(assign, cache, scale, hidden, ids, weights):
    tokens = LINE * hidden.shape[0] * STEPS
    args = (assign, cache, scale, hidden, ids, weights)
    shapes = ((PLANE * KEEP, SIDE), (PLANE * KEEP, SIDE), (tokens, WIDE))
    return pl.pallas_call(
        prepare_kernel,
        grid=(1,),
        out_shape=[jax.ShapeDtypeStruct(shape, jnp.bfloat16) for shape in shapes],
        in_specs=[whole(a.shape) for a in args],
        out_specs=[whole(shape) for shape in shapes],
        compiler_params=pltpu.CompilerParams(vmem_limit_bytes=58 * MIB),
        name="prepare",
    )(*args)


def finish_kernel(
    assign_ref, lengths_ref, gathered_ref, query_ref, fresh_ref, out_ref, moe_ref
):
    group, ep_index = lax.axis_index("pool"), lax.axis_index(EP_AXES)
    slot_dev, rows = query_ref.shape[:2]
    lines = gathered_ref.shape[0]
    parts = PLANE // SPREAD
    positions = parts * lines
    blocks = LAT // QB
    device = slot_dev * STEPS
    total = sum(
        gathered_ref[pl.ds(z * device, device), pl.ds(0, D)].astype(jnp.float32) for z in range(LINE)
    ).astype(jnp.bfloat16)
    for b in range(slot_dev):
        moe_ref[b] = total[b * STEPS : (b + 1) * STEPS]
    assigned = jnp.where(group == 0, assign_ref[1:2, :], assign_ref[0:1, :])
    lengths = jnp.where(group == 0, lengths_ref[1:2, :], lengths_ref[0:1, :])
    lane = lax.broadcasted_iota(jnp.int32, (rows, positions), 1)
    place = lane // lines * SPREAD + lane % SPREAD
    position = place // FOUR * (LINE * FOUR) + lane % lines // SPREAD * FOUR + place % FOUR
    new = 16
    step = lax.broadcasted_iota(jnp.int32, (rows, new), 0) // (rows // STEPS)
    token = lax.broadcasted_iota(jnp.int32, (rows, new), 1)
    by_rows = (((1,), (1,)), ((), ()))
    for b in range(slot_dev):
        slot = ep_index * slot_dev + b
        length = jnp.sum(jnp.where(assigned == slot, lengths, 0), axis=1, keepdims=True)
        keys = jnp.concatenate(
            [
                gathered_ref[:, pl.ds(D + (b * parts + part) * ROW, ROW)]
                for part in range(parts)
            ],
            axis=0,
        )
        scale = keys[:, LAT:].astype(jnp.float32).T[ROPE : ROPE + blocks]
        score = lax.dot_general(
            query_ref[b, :, pl.ds(LAT, ROPE)],
            keys[:, LAT : LAT + ROPE],
            by_rows,
            preferred_element_type=jnp.float32,
        )
        for n in range(blocks):
            part = lax.dot_general(
                query_ref[b, :, pl.ds(n * QB, QB)],
                keys[:, n * QB : (n + 1) * QB],
                by_rows,
                preferred_element_type=jnp.float32,
            )
            score = score + part * scale[n : n + 1]
        score = jnp.where(position < length, score * SCORE_SCALE, NEGATIVE)
        fresh = jnp.concatenate(
            [fresh_ref[b].astype(jnp.float32), jnp.zeros((new - STEPS, LAT + ROPE), jnp.float32)],
            axis=0,
        ).astype(jnp.bfloat16)
        score_fresh = lax.dot_general(
            query_ref[b], fresh, by_rows, preferred_element_type=jnp.float32
        )
        score_fresh = jnp.where(token <= step, score_fresh * SCORE_SCALE, NEGATIVE)
        top = jnp.maximum(
            jnp.max(score, axis=1, keepdims=True), jnp.max(score_fresh, axis=1, keepdims=True)
        )
        exp_cache, exp_fresh = jnp.exp(score - top), jnp.exp(score_fresh - top)
        summed = jnp.sum(exp_cache, axis=1, keepdims=True)
        summed = summed + jnp.sum(exp_fresh, axis=1, keepdims=True)
        prob = exp_cache / summed
        weight_fresh = (exp_fresh / summed).astype(jnp.bfloat16)
        for n in range(blocks):
            columns = slice(n * QB, (n + 1) * QB)
            weight = (prob * scale[n : n + 1]).astype(jnp.bfloat16)
            latent = jnp.dot(weight, keys[:, columns], preferred_element_type=jnp.float32)
            latent = latent + jnp.dot(
                weight_fresh, fresh[:, columns], preferred_element_type=jnp.float32
            )
            out_ref[b, :, pl.ds(n * QB, QB)] = latent.astype(jnp.bfloat16)


def finish(assign, lengths, gathered, queries, fresh):
    slot_dev, rows = queries.shape[:2]
    vmem = pl.BlockSpec(memory_space=pltpu.VMEM)
    return pl.pallas_call(
        finish_kernel,
        out_shape=(
            jax.ShapeDtypeStruct((slot_dev, rows, LAT), jnp.bfloat16),
            jax.ShapeDtypeStruct((slot_dev, STEPS, D), jnp.bfloat16),
        ),
        in_specs=[vmem] * 5,
        out_specs=(vmem, vmem),
        compiler_params=pltpu.CompilerParams(vmem_limit_bytes=16 * MIB),
        name="finish",
    )(assign, lengths, gathered, queries, fresh)


def on_device(
    cache,
    cache_scale,
    lengths,
    assign,
    queries,
    new_kv,
    hidden,
    expert_ids,
    expert_weights,
    gate_w,
    up_w,
    down_w,
):
    slot_dev, heads = queries.shape[1], queries.shape[3]
    token_count = slot_dev * STEPS
    kept, given, token_rows = prepare(
        assign,
        cache[0, :, 0, :].T,
        cache_scale[0, :, 0, :].T,
        hidden[0],
        expert_ids[0],
        expert_weights[0],
    )
    given = lax.ppermute(given, "pool", [(0, 1), (1, 0)])
    line = lax.all_to_all(
        token_rows.reshape(LINE, token_count, WIDE), LINE_AXES, 0, 0, tiled=True
    ).reshape(LINE * token_count, WIDE)
    line, given = lax.optimization_barrier((line, given))

    sent, mix = dispatch(line, kept, given)
    taken = lax.all_to_all(
        sent.reshape(2 * PLANE, KEEP, D + SIDE), CROSS_AXES, 0, 0, tiled=True
    ).reshape(2 * PLANE * KEEP, D + SIDE)

    served = expert(taken, gate_w[0], up_w[0], down_w[0])

    served, taken = lax.optimization_barrier((served, taken))
    beside = turned(taken)
    served, beside = lax.optimization_barrier((served, beside))
    back = lax.all_to_all(
        served.reshape(2 * PLANE, KEEP, D), CROSS_AXES, 0, 0, tiled=True
    ).reshape(2 * PLANE * KEEP, D)

    mixed = combine(mix, back, beside)
    gathered = lax.all_to_all(
        mixed.reshape(LINE, token_count, -1), LINE_AXES, 0, 0, tiled=True
    ).reshape(mixed.shape)
    context, moe_out = finish(
        assign,
        lengths,
        gathered,
        queries[0].reshape(slot_dev, STEPS * heads, -1),
        new_kv[0],
    )
    return (
        context.reshape(1, slot_dev, STEPS, heads, LAT),
        moe_out.reshape(1, slot_dev, STEPS, D),
    )


def solution(mesh):
    fine = Mesh(
        mesh.devices.reshape(2, Y, XH, LINE, ZL, CORE), ("pool", "y", "xh", "zh", "zl", "core")
    )
    return jax.shard_map(
        on_device,
        mesh=fine,
        in_specs=(
            P("pool", None, EP_AXES, None),
            P("pool", None, EP_AXES, None),
            P(),
            P(),
            P("pool", EP_AXES, None, None, None),
            P("pool", EP_AXES, None, None),
            P("pool", EP_AXES, None, None),
            P("pool", EP_AXES, None, None),
            P("pool", EP_AXES, None, None),
            P(EP_AXES, None, "pool"),
            P(EP_AXES, None, "pool"),
            P(EP_AXES, "pool", None),
        ),
        out_specs=(P("pool", EP_AXES, None, None, None), P("pool", EP_AXES, None, None)),
        check_vma=False,
    )
```

```python
import jax
import jax.numpy as jnp
from jax import lax
from jax.experimental import pallas as pl
from jax.experimental.pallas import tpu as pltpu
from jax.sharding import Mesh, PartitionSpec as P

STEPS = 4
LAT = 512
ROPE = 64
QB = 128
D = 3584
TOP = 8
CAP = 2

Y, XH, LINE, ZL, CORE = 4, 2, 4, 2, 2
FOUR = ZL * CORE
PLANE = Y * XH * FOUR
KEEP = LINE * CAP
ROW = 640
SIDE = 384
SPREAD = 8

SCORE_SCALE = 192.0 ** (-0.5)
NEGATIVE = -1e30

LINE_AXES = "zh"
CROSS_AXES = ("pool", "y", "xh", "zl", "core")
EP_AXES = ("y", "xh", "zh", "zl", "core")


WIDE = D + 128
BLOCK = 512
MIB = 1 << 20


def whole(shape):
    return pl.BlockSpec(shape, lambda i: (0,) * len(shape))


def dispatch_kernel(line_ref, kept_ref, given_ref, sent_ref, mix_ref, done):
    group, zh = lax.axis_index("pool"), lax.axis_index(LINE_AXES)
    count = PLANE * KEEP
    copies = []
    for index, (half, ref) in enumerate(((group, given_ref), (1 - group, kept_ref))):
        top = pl.multiple_of(half * count, count)
        target = sent_ref.at[pl.ds(top, count), pl.ds(D, SIDE)]
        copies.append(pltpu.make_async_copy(ref, target, done.at[index]))
        copies[index].start()
    tokens = line_ref.shape[0]
    routing = jnp.concatenate(
        [line_ref[:, pl.ds(D, 128)].astype(jnp.float32), jnp.zeros((128 - tokens, 128), jnp.float32)],
        axis=0,
    ).T[:, :tokens]
    place = lax.broadcasted_iota(jnp.int32, (PLANE, tokens), 0)
    expert_at = place // FOUR * (LINE * FOUR) + zh * FOUR + place % FOUR
    hit = jnp.zeros((PLANE, tokens), jnp.float32)
    share = jnp.zeros((PLANE, tokens), jnp.float32)
    for k in range(TOP):
        weight = sum(routing[TOP * part + k : TOP * part + k + 1] for part in (1, 2, 3))
        named = routing[k : k + 1].astype(jnp.int32) == expert_at
        hit = hit + jnp.where(named, 1.0, 0.0)
        share = share + jnp.where(named, weight, 0.0)
    token = lax.broadcasted_iota(jnp.int32, (tokens, tokens), 0)
    other = lax.broadcasted_iota(jnp.int32, (tokens, tokens), 1)
    rank = jnp.dot(
        hit.astype(jnp.bfloat16),
        jnp.where(token < other, 1.0, 0.0).astype(jnp.bfloat16),
        preferred_element_type=jnp.float32,
    )
    rank = jnp.where(hit > 0.0, rank, -1.0).astype(jnp.int32)
    seat = lax.broadcasted_iota(jnp.int32, (KEEP, tokens), 0)
    chosen = [seat == rank[e : e + 1] for e in range(PLANE)]
    choose = jnp.concatenate([jnp.where(c, 1.0, 0.0) for c in chosen], axis=0)
    choose = choose.astype(jnp.bfloat16)
    mix = jnp.concatenate(
        [jnp.where(chosen[e], share[e : e + 1], 0.0) for e in range(PLANE)], axis=0
    )
    high = mix.astype(jnp.bfloat16)
    low = (mix - high.astype(jnp.float32)).astype(jnp.bfloat16)
    same = jnp.where(token == other, 1.0, 0.0).astype(jnp.bfloat16)
    for index, part in enumerate((high, low)):
        across = lax.dot_general(
            same, part, (((1,), (1,)), ((), ())), preferred_element_type=jnp.float32
        ).astype(jnp.bfloat16)
        mix_ref[index] = jnp.concatenate([across, across], axis=1)
    for start in range(0, D, BLOCK):
        columns = pl.ds(start, BLOCK)
        rows = jnp.dot(choose, line_ref[:, columns], preferred_element_type=jnp.float32)
        rows = rows.astype(jnp.bfloat16)
        sent_ref[pl.ds(0, count), columns] = rows
        sent_ref[pl.ds(count, count), columns] = rows
    for copy in copies:
        copy.wait()


def dispatch(line, kept, given):
    tokens = line.shape[0]
    count = 2 * PLANE * KEEP
    vmem = pl.BlockSpec(memory_space=pltpu.VMEM)
    return pl.pallas_call(
        dispatch_kernel,
        out_shape=(
            jax.ShapeDtypeStruct((count, D + SIDE), jnp.bfloat16),
            jax.ShapeDtypeStruct((2, tokens, count), jnp.bfloat16),
        ),
        in_specs=[vmem, pl.BlockSpec(memory_space=pltpu.HBM), pl.BlockSpec(memory_space=pl.ANY)],
        out_specs=(vmem, vmem),
        scratch_shapes=[pltpu.SemaphoreType.DMA((2,))],
        compiler_params=pltpu.CompilerParams(vmem_limit_bytes=24 * MIB),
        cost_estimate=pl.CostEstimate(
            flops=2 * count * tokens * D, bytes_accessed=8 * count * D, transcendentals=0
        ),
        name="dispatch",
    )(line, kept, given)


def turn_kernel(one_ref, two_ref, three_ref, out_ref):
    rows = out_ref.shape[0]
    group = SPREAD * KEEP
    to = lax.broadcasted_iota(jnp.int32, (rows, group), 0)
    at = lax.broadcasted_iota(jnp.int32, (rows, group), 1)
    first = to % SPREAD * KEEP + to // SPREAD
    for index in range(out_ref.shape[1] // ROW):
        block = pl.ds(index * group, group)
        three = jnp.concatenate([r[block, :] for r in (one_ref, two_ref, three_ref)], axis=1)
        for part, (start, width) in enumerate(((0, SIDE), (SIDE, ROW - SIDE))):
            turn = jnp.where(at == first + part * LINE, 1.0, 0.0).astype(jnp.bfloat16)
            moved = jnp.dot(turn, three[:, :width], preferred_element_type=jnp.float32)
            out_ref[:, pl.ds(index * ROW + start, width)] = moved.astype(jnp.bfloat16)


def turned(taken):
    rows = taken.shape[0]
    shape = (LINE * SPREAD, rows // (SPREAD * KEEP) * ROW)
    return pl.pallas_call(
        turn_kernel,
        grid=(1,),
        out_shape=jax.ShapeDtypeStruct(shape, jnp.bfloat16),
        in_specs=[
            pl.BlockSpec((rows, 128), lambda i, at=at: (0, D // 128 + at)) for at in range(3)
        ],
        out_specs=whole(shape),
        compiler_params=pltpu.CompilerParams(vmem_limit_bytes=12 * MIB),
        name="turned",
    )(taken, taken, taken)


def inner_kernel(taken_ref, gate_ref, up_ref, inner_ref):
    for start in range(0, inner_ref.shape[1], 256):
        columns = pl.ds(start, 256)
        rows = taken_ref[:, pl.ds(0, D)]
        gate = jnp.dot(rows, gate_ref[:, columns], preferred_element_type=jnp.float32)
        up = jnp.dot(rows, up_ref[:, columns], preferred_element_type=jnp.float32)
        inner_ref[:, columns] = (jax.nn.silu(gate) * up).astype(jnp.bfloat16)


def served_kernel(inner_ref, down_ref, out_ref):
    for start in range(0, D, BLOCK):
        columns = pl.ds(start, BLOCK)
        out_ref[:, columns] = jnp.dot(
            inner_ref[...], down_ref[:, columns], preferred_element_type=jnp.float32
        ).astype(jnp.bfloat16)


def expert(taken, gate, up, down):
    count, width = taken.shape[0], gate.shape[1]
    vmem = pl.BlockSpec(memory_space=pltpu.VMEM)
    inner = pl.pallas_call(
        inner_kernel,
        out_shape=jax.ShapeDtypeStruct((count, width), jnp.bfloat16),
        in_specs=[vmem, vmem, vmem],
        out_specs=vmem,
        compiler_params=pltpu.CompilerParams(vmem_limit_bytes=20 * MIB),
        cost_estimate=pl.CostEstimate(
            flops=4 * count * width * D,
            bytes_accessed=4 * width * D + 2 * count * (D + width),
            transcendentals=count * width,
        ),
        name="inner",
    )(taken, gate, up)
    return pl.pallas_call(
        served_kernel,
        out_shape=jax.ShapeDtypeStruct((count, D), jnp.bfloat16),
        in_specs=[vmem, vmem],
        out_specs=vmem,
        compiler_params=pltpu.CompilerParams(vmem_limit_bytes=16 * MIB),
        cost_estimate=pl.CostEstimate(
            flops=2 * count * width * D,
            bytes_accessed=2 * width * D + 2 * count * (D + width),
            transcendentals=0,
        ),
        name="served",
    )(inner, down)


def combine_kernel(mix_ref, back_ref, beside_ref, out_ref):
    tokens = mix_ref.shape[1]
    mix = jnp.concatenate([mix_ref[0], mix_ref[1]], axis=0)
    for start in range(0, D, BLOCK):
        columns = pl.ds(start, BLOCK)
        both = jnp.dot(mix, back_ref[:, columns], preferred_element_type=jnp.float32)
        out_ref[:, columns] = (both[:tokens] + both[tokens:]).astype(jnp.bfloat16)
    out_ref[:, pl.ds(D, beside_ref.shape[1])] = beside_ref[...]


def combine(mix, back, beside):
    vmem = pl.BlockSpec(memory_space=pltpu.VMEM)
    return pl.pallas_call(
        combine_kernel,
        out_shape=jax.ShapeDtypeStruct((mix.shape[1], D + beside.shape[1]), jnp.bfloat16),
        in_specs=[vmem, vmem, vmem],
        out_specs=vmem,
        compiler_params=pltpu.CompilerParams(vmem_limit_bytes=12 * MIB),
        name="combine",
    )(mix, back, beside)


def prepare_kernel(
    assign_ref, cache_ref, scale_ref, hidden_ref, ids_ref, weights_ref,
    kept_ref, given_ref, tokens_ref,
):
    group = lax.axis_index("pool")
    slot_dev = hidden_ref.shape[0]
    requests = assign_ref.shape[1]
    hidden = [hidden_ref[b].astype(jnp.float32) for b in range(slot_dev)]
    hidden = jnp.concatenate(hidden, axis=0)
    ids = jnp.concatenate([ids_ref[b].astype(jnp.float32) for b in range(slot_dev)], axis=0)
    rest = jnp.concatenate([weights_ref[b] for b in range(slot_dev)], axis=0)
    terms = [ids.astype(jnp.bfloat16)]
    for _ in range(3):
        term = rest.astype(jnp.bfloat16)
        rest = rest - term.astype(jnp.float32)
        terms.append(term)
    at = lax.broadcasted_iota(jnp.int32, (TOP, WIDE - D), 0)
    lane = lax.broadcasted_iota(jnp.int32, (TOP, WIDE - D), 1)
    routing = sum(
        jnp.dot(
            term,
            jnp.where(lane == at + TOP * index, 1.0, 0.0).astype(jnp.bfloat16),
            preferred_element_type=jnp.float32,
        )
        for index, term in enumerate(terms)
    )
    row = jnp.concatenate([hidden, routing], axis=1)
    tokens_ref[...] = jnp.concatenate([row] * LINE, axis=0).astype(jnp.bfloat16)
    row = jnp.where(group == 0, assign_ref[0:1, :], assign_ref[1:2, :])
    tail = jnp.concatenate(
        [
            scale_ref[...].astype(jnp.float32),
            jnp.zeros((ROW - LAT - ROPE - LAT // QB, requests), jnp.float32),
        ],
        axis=0,
    ).astype(jnp.bfloat16)
    stored = jnp.concatenate([cache_ref[...], tail], axis=0)
    at = lax.broadcasted_iota(jnp.int32, (PLANE * KEEP, requests), 0)
    place, zh = at // KEEP, at % LINE
    slot = (place // FOUR * (LINE * FOUR) + zh * FOUR + place % FOUR) * slot_dev
    head = lax.broadcasted_iota(jnp.int32, (PLANE * KEEP, SIDE), 0) % KEEP < LINE
    for half, ref in ((group, kept_ref), (1 - group, given_ref)):
        choose = jnp.where(slot + half == row, 1.0, 0.0).astype(jnp.bfloat16)
        found = lax.dot_general(
            choose, stored, (((1,), (1,)), ((), ())), preferred_element_type=jnp.float32
        )
        tail = jnp.concatenate(
            [found[:, SIDE:], jnp.zeros((PLANE * KEEP, 2 * SIDE - ROW), jnp.float32)], axis=1
        )
        ref[...] = jnp.where(head, found[:, :SIDE], tail).astype(jnp.bfloat16)


def prepare(assign, cache, scale, hidden, ids, weights):
    tokens = LINE * hidden.shape[0] * STEPS
    args = (assign, cache, scale, hidden, ids, weights)
    shapes = ((PLANE * KEEP, SIDE), (PLANE * KEEP, SIDE), (tokens, WIDE))
    return pl.pallas_call(
        prepare_kernel,
        grid=(1,),
        out_shape=[jax.ShapeDtypeStruct(shape, jnp.bfloat16) for shape in shapes],
        in_specs=[whole(a.shape) for a in args],
        out_specs=[whole(shape) for shape in shapes],
        compiler_params=pltpu.CompilerParams(vmem_limit_bytes=58 * MIB),
        name="prepare",
    )(*args)


def finish_kernel(
    assign_ref, lengths_ref, gathered_ref, query_ref, fresh_ref, out_ref, moe_ref
):
    group, ep_index = lax.axis_index("pool"), lax.axis_index(EP_AXES)
    slot_dev, rows = query_ref.shape[:2]
    lines = gathered_ref.shape[0]
    parts = PLANE // SPREAD
    positions = parts * lines
    blocks = LAT // QB
    device = slot_dev * STEPS
    total = sum(
        gathered_ref[pl.ds(z * device, device), pl.ds(0, D)].astype(jnp.float32) for z in range(LINE)
    ).astype(jnp.bfloat16)
    for b in range(slot_dev):
        moe_ref[b] = total[b * STEPS : (b + 1) * STEPS]
    assigned = jnp.where(group == 0, assign_ref[1:2, :], assign_ref[0:1, :])
    lengths = jnp.where(group == 0, lengths_ref[1:2, :], lengths_ref[0:1, :])
    lane = lax.broadcasted_iota(jnp.int32, (rows, positions), 1)
    place = lane // lines * SPREAD + lane % SPREAD
    position = place // FOUR * (LINE * FOUR) + lane % lines // SPREAD * FOUR + place % FOUR
    new = 16
    step = lax.broadcasted_iota(jnp.int32, (rows, new), 0) // (rows // STEPS)
    token = lax.broadcasted_iota(jnp.int32, (rows, new), 1)
    by_rows = (((1,), (1,)), ((), ()))
    for b in range(slot_dev):
        slot = ep_index * slot_dev + b
        length = jnp.sum(jnp.where(assigned == slot, lengths, 0), axis=1, keepdims=True)
        keys = jnp.concatenate(
            [
                gathered_ref[:, pl.ds(D + (b * parts + part) * ROW, ROW)]
                for part in range(parts)
            ],
            axis=0,
        )
        scale = keys[:, LAT:].astype(jnp.float32).T[ROPE : ROPE + blocks]
        score = lax.dot_general(
            query_ref[b, :, pl.ds(LAT, ROPE)],
            keys[:, LAT : LAT + ROPE],
            by_rows,
            preferred_element_type=jnp.float32,
        )
        for n in range(blocks):
            part = lax.dot_general(
                query_ref[b, :, pl.ds(n * QB, QB)],
                keys[:, n * QB : (n + 1) * QB],
                by_rows,
                preferred_element_type=jnp.float32,
            )
            score = score + part * scale[n : n + 1]
        score = jnp.where(position < length, score * SCORE_SCALE, NEGATIVE)
        fresh = jnp.concatenate(
            [fresh_ref[b].astype(jnp.float32), jnp.zeros((new - STEPS, LAT + ROPE), jnp.float32)],
            axis=0,
        ).astype(jnp.bfloat16)
        score_fresh = lax.dot_general(
            query_ref[b], fresh, by_rows, preferred_element_type=jnp.float32
        )
        score_fresh = jnp.where(token <= step, score_fresh * SCORE_SCALE, NEGATIVE)
        top = jnp.maximum(
            jnp.max(score, axis=1, keepdims=True), jnp.max(score_fresh, axis=1, keepdims=True)
        )
        exp_cache, exp_fresh = jnp.exp(score - top), jnp.exp(score_fresh - top)
        summed = jnp.sum(exp_cache, axis=1, keepdims=True)
        summed = summed + jnp.sum(exp_fresh, axis=1, keepdims=True)
        prob = exp_cache / summed
        weight_fresh = (exp_fresh / summed).astype(jnp.bfloat16)
        for n in range(blocks):
            columns = slice(n * QB, (n + 1) * QB)
            weight = (prob * scale[n : n + 1]).astype(jnp.bfloat16)
            latent = jnp.dot(weight, keys[:, columns], preferred_element_type=jnp.float32)
            latent = latent + jnp.dot(
                weight_fresh, fresh[:, columns], preferred_element_type=jnp.float32
            )
            out_ref[b, :, pl.ds(n * QB, QB)] = latent.astype(jnp.bfloat16)


def finish(assign, lengths, gathered, queries, fresh):
    slot_dev, rows = queries.shape[:2]
    vmem = pl.BlockSpec(memory_space=pltpu.VMEM)
    return pl.pallas_call(
        finish_kernel,
        out_shape=(
            jax.ShapeDtypeStruct((slot_dev, rows, LAT), jnp.bfloat16),
            jax.ShapeDtypeStruct((slot_dev, STEPS, D), jnp.bfloat16),
        ),
        in_specs=[vmem] * 5,
        out_specs=(vmem, vmem),
        compiler_params=pltpu.CompilerParams(vmem_limit_bytes=16 * MIB),
        name="finish",
    )(assign, lengths, gathered, queries, fresh)


def on_device(
    cache,
    cache_scale,
    lengths,
    assign,
    queries,
    new_kv,
    hidden,
    expert_ids,
    expert_weights,
    gate_w,
    up_w,
    down_w,
):
    slot_dev, heads = queries.shape[1], queries.shape[3]
    token_count = slot_dev * STEPS
    kept, given, token_rows = prepare(
        assign,
        cache[0, :, 0, :].T,
        cache_scale[0, :, 0, :].T,
        hidden[0],
        expert_ids[0],
        expert_weights[0],
    )
    given = lax.ppermute(given, "pool", [(0, 1), (1, 0)])
    line = lax.all_to_all(
        token_rows.reshape(LINE, token_count, WIDE), LINE_AXES, 0, 0, tiled=True
    ).reshape(LINE * token_count, WIDE)
    line, given = lax.optimization_barrier((line, given))

    sent, mix = dispatch(line, kept, given)
    taken = lax.all_to_all(
        sent.reshape(2 * PLANE, KEEP, D + SIDE), CROSS_AXES, 0, 0, tiled=True
    ).reshape(2 * PLANE * KEEP, D + SIDE)

    served = expert(taken, gate_w[0], up_w[0], down_w[0])

    served, taken = lax.optimization_barrier((served, taken))
    beside = turned(taken)
    served, beside = lax.optimization_barrier((served, beside))
    back = lax.all_to_all(
        served.reshape(2 * PLANE, KEEP, D), CROSS_AXES, 0, 0, tiled=True
    ).reshape(2 * PLANE * KEEP, D)

    mixed = combine(mix, back, beside)
    gathered = lax.all_to_all(
        mixed.reshape(LINE, token_count, -1), LINE_AXES, 0, 0, tiled=True
    ).reshape(mixed.shape)
    context, moe_out = finish(
        assign,
        lengths,
        gathered,
        queries[0].reshape(slot_dev, STEPS * heads, -1),
        new_kv[0],
    )
    return (
        context.reshape(1, slot_dev, STEPS, heads, LAT),
        moe_out.reshape(1, slot_dev, STEPS, D),
    )


def solution(mesh):
    fine = Mesh(
        mesh.devices.reshape(2, Y, XH, LINE, ZL, CORE), ("pool", "y", "xh", "zh", "zl", "core")
    )
    return jax.shard_map(
        on_device,
        mesh=fine,
        in_specs=(
            P("pool", None, EP_AXES, None),
            P("pool", None, EP_AXES, None),
            P(),
            P(),
            P("pool", EP_AXES, None, None, None),
            P("pool", EP_AXES, None, None),
            P("pool", EP_AXES, None, None),
            P("pool", EP_AXES, None, None),
            P("pool", EP_AXES, None, None),
            P(EP_AXES, None, "pool"),
            P(EP_AXES, None, "pool"),
            P(EP_AXES, "pool", None),
        ),
        out_specs=(P("pool", EP_AXES, None, None, None), P("pool", EP_AXES, None, None)),
        check_vma=False,
    )
```

```python
import jax
import jax.numpy as jnp
from jax import lax
from jax.experimental import pallas as pl
from jax.experimental.pallas import tpu as pltpu
from jax.sharding import Mesh, PartitionSpec as P

STEPS = 4
LAT = 512
ROPE = 64
QB = 128
D = 3584
TOP = 8
CAP = 2

Y, XH, LINE, ZL, CORE = 4, 2, 4, 2, 2
FOUR = ZL * CORE
PLANE = Y * XH * FOUR
KEEP = LINE * CAP
ROW = 640
SIDE = 384
SPREAD = 8

SCORE_SCALE = 192.0 ** (-0.5)
NEGATIVE = -1e30

LINE_AXES = "zh"
CROSS_AXES = ("pool", "y", "xh", "zl", "core")
EP_AXES = ("y", "xh", "zh", "zl", "core")


WIDE = D + 128
BLOCK = 512
MIB = 1 << 20


def whole(shape):
    return pl.BlockSpec(shape, lambda i: (0,) * len(shape))


def dispatch_kernel(line_ref, kept_ref, given_ref, sent_ref, mix_ref, done):
    group, zh = lax.axis_index("pool"), lax.axis_index(LINE_AXES)
    count = PLANE * KEEP
    copies = []
    for index, (half, ref) in enumerate(((group, given_ref), (1 - group, kept_ref))):
        top = pl.multiple_of(half * count, count)
        target = sent_ref.at[pl.ds(top, count), pl.ds(D, SIDE)]
        copies.append(pltpu.make_async_copy(ref, target, done.at[index]))
        copies[index].start()
    tokens = line_ref.shape[0]
    routing = jnp.concatenate(
        [line_ref[:, pl.ds(D, 128)].astype(jnp.float32), jnp.zeros((128 - tokens, 128), jnp.float32)],
        axis=0,
    ).T[:, :tokens]
    place = lax.broadcasted_iota(jnp.int32, (PLANE, tokens), 0)
    expert_at = place // FOUR * (LINE * FOUR) + zh * FOUR + place % FOUR
    hit = jnp.zeros((PLANE, tokens), jnp.float32)
    share = jnp.zeros((PLANE, tokens), jnp.float32)
    for k in range(TOP):
        weight = sum(routing[TOP * part + k : TOP * part + k + 1] for part in (1, 2, 3))
        named = routing[k : k + 1].astype(jnp.int32) == expert_at
        hit = hit + jnp.where(named, 1.0, 0.0)
        share = share + jnp.where(named, weight, 0.0)
    token = lax.broadcasted_iota(jnp.int32, (tokens, tokens), 0)
    other = lax.broadcasted_iota(jnp.int32, (tokens, tokens), 1)
    rank = jnp.dot(
        hit.astype(jnp.bfloat16),
        jnp.where(token < other, 1.0, 0.0).astype(jnp.bfloat16),
        preferred_element_type=jnp.float32,
    )
    rank = jnp.where(hit > 0.0, rank, -1.0).astype(jnp.int32)
    seat = lax.broadcasted_iota(jnp.int32, (KEEP, tokens), 0)
    chosen = [seat == rank[e : e + 1] for e in range(PLANE)]
    choose = jnp.concatenate([jnp.where(c, 1.0, 0.0) for c in chosen], axis=0)
    choose = choose.astype(jnp.bfloat16)
    mix = jnp.concatenate(
        [jnp.where(chosen[e], share[e : e + 1], 0.0) for e in range(PLANE)], axis=0
    )
    high = mix.astype(jnp.bfloat16)
    low = (mix - high.astype(jnp.float32)).astype(jnp.bfloat16)
    same = jnp.where(token == other, 1.0, 0.0).astype(jnp.bfloat16)
    for index, part in enumerate((high, low)):
        across = lax.dot_general(
            same, part, (((1,), (1,)), ((), ())), preferred_element_type=jnp.float32
        ).astype(jnp.bfloat16)
        mix_ref[index] = jnp.concatenate([across, across], axis=1)
    for start in range(0, D, BLOCK):
        columns = pl.ds(start, BLOCK)
        rows = jnp.dot(choose, line_ref[:, columns], preferred_element_type=jnp.float32)
        rows = rows.astype(jnp.bfloat16)
        sent_ref[pl.ds(0, count), columns] = rows
        sent_ref[pl.ds(count, count), columns] = rows
    for copy in copies:
        copy.wait()


def dispatch(line, kept, given):
    tokens = line.shape[0]
    count = 2 * PLANE * KEEP
    vmem = pl.BlockSpec(memory_space=pltpu.VMEM)
    return pl.pallas_call(
        dispatch_kernel,
        out_shape=(
            jax.ShapeDtypeStruct((count, D + SIDE), jnp.bfloat16),
            jax.ShapeDtypeStruct((2, tokens, count), jnp.bfloat16),
        ),
        in_specs=[vmem, pl.BlockSpec(memory_space=pltpu.HBM), pl.BlockSpec(memory_space=pl.ANY)],
        out_specs=(vmem, vmem),
        scratch_shapes=[pltpu.SemaphoreType.DMA((2,))],
        compiler_params=pltpu.CompilerParams(vmem_limit_bytes=24 * MIB),
        cost_estimate=pl.CostEstimate(
            flops=2 * count * tokens * D, bytes_accessed=8 * count * D, transcendentals=0
        ),
        name="dispatch",
    )(line, kept, given)


def turn_kernel(one_ref, two_ref, three_ref, out_ref):
    rows = out_ref.shape[0]
    group = SPREAD * KEEP
    to = lax.broadcasted_iota(jnp.int32, (rows, group), 0)
    at = lax.broadcasted_iota(jnp.int32, (rows, group), 1)
    first = to % SPREAD * KEEP + to // SPREAD
    for index in range(out_ref.shape[1] // ROW):
        block = pl.ds(index * group, group)
        three = jnp.concatenate([r[block, :] for r in (one_ref, two_ref, three_ref)], axis=1)
        for part, (start, width) in enumerate(((0, SIDE), (SIDE, ROW - SIDE))):
            turn = jnp.where(at == first + part * LINE, 1.0, 0.0).astype(jnp.bfloat16)
            moved = jnp.dot(turn, three[:, :width], preferred_element_type=jnp.float32)
            out_ref[:, pl.ds(index * ROW + start, width)] = moved.astype(jnp.bfloat16)


def turned(taken):
    rows = taken.shape[0]
    shape = (LINE * SPREAD, rows // (SPREAD * KEEP) * ROW)
    return pl.pallas_call(
        turn_kernel,
        grid=(1,),
        out_shape=jax.ShapeDtypeStruct(shape, jnp.bfloat16),
        in_specs=[
            pl.BlockSpec((rows, 128), lambda i, at=at: (0, D // 128 + at)) for at in range(3)
        ],
        out_specs=whole(shape),
        compiler_params=pltpu.CompilerParams(vmem_limit_bytes=12 * MIB),
        name="turned",
    )(taken, taken, taken)


def inner_kernel(taken_ref, gate_ref, up_ref, inner_ref):
    for start in range(0, inner_ref.shape[1], 256):
        columns = pl.ds(start, 256)
        rows = taken_ref[:, pl.ds(0, D)]
        gate = jnp.dot(rows, gate_ref[:, columns], preferred_element_type=jnp.float32)
        up = jnp.dot(rows, up_ref[:, columns], preferred_element_type=jnp.float32)
        inner_ref[:, columns] = (jax.nn.silu(gate) * up).astype(jnp.bfloat16)


def served_kernel(inner_ref, down_ref, out_ref):
    for start in range(0, D, BLOCK):
        columns = pl.ds(start, BLOCK)
        out_ref[:, columns] = jnp.dot(
            inner_ref[...], down_ref[:, columns], preferred_element_type=jnp.float32
        ).astype(jnp.bfloat16)


def expert(taken, gate, up, down):
    count, width = taken.shape[0], gate.shape[1]
    vmem = pl.BlockSpec(memory_space=pltpu.VMEM)
    inner = pl.pallas_call(
        inner_kernel,
        out_shape=jax.ShapeDtypeStruct((count, width), jnp.bfloat16),
        in_specs=[vmem, vmem, vmem],
        out_specs=vmem,
        compiler_params=pltpu.CompilerParams(vmem_limit_bytes=20 * MIB),
        cost_estimate=pl.CostEstimate(
            flops=4 * count * width * D,
            bytes_accessed=4 * width * D + 2 * count * (D + width),
            transcendentals=count * width,
        ),
        name="inner",
    )(taken, gate, up)
    return pl.pallas_call(
        served_kernel,
        out_shape=jax.ShapeDtypeStruct((count, D), jnp.bfloat16),
        in_specs=[vmem, vmem],
        out_specs=vmem,
        compiler_params=pltpu.CompilerParams(vmem_limit_bytes=16 * MIB),
        cost_estimate=pl.CostEstimate(
            flops=2 * count * width * D,
            bytes_accessed=2 * width * D + 2 * count * (D + width),
            transcendentals=0,
        ),
        name="served",
    )(inner, down)


def combine_kernel(mix_ref, back_ref, beside_ref, out_ref):
    tokens = mix_ref.shape[1]
    mix = jnp.concatenate([mix_ref[0], mix_ref[1]], axis=0)
    for start in range(0, D, BLOCK):
        columns = pl.ds(start, BLOCK)
        both = jnp.dot(mix, back_ref[:, columns], preferred_element_type=jnp.float32)
        out_ref[:, columns] = (both[:tokens] + both[tokens:]).astype(jnp.bfloat16)
    out_ref[:, pl.ds(D, beside_ref.shape[1])] = beside_ref[...]


def combine(mix, back, beside):
    vmem = pl.BlockSpec(memory_space=pltpu.VMEM)
    return pl.pallas_call(
        combine_kernel,
        out_shape=jax.ShapeDtypeStruct((mix.shape[1], D + beside.shape[1]), jnp.bfloat16),
        in_specs=[vmem, vmem, vmem],
        out_specs=vmem,
        compiler_params=pltpu.CompilerParams(vmem_limit_bytes=12 * MIB),
        name="combine",
    )(mix, back, beside)


def prepare_kernel(
    assign_ref, cache_ref, scale_ref, hidden_ref, ids_ref, weights_ref,
    kept_ref, given_ref, tokens_ref,
):
    group = lax.axis_index("pool")
    slot_dev = hidden_ref.shape[0]
    requests = assign_ref.shape[1]
    hidden = [hidden_ref[b].astype(jnp.float32) for b in range(slot_dev)]
    hidden = jnp.concatenate(hidden, axis=0)
    ids = jnp.concatenate([ids_ref[b].astype(jnp.float32) for b in range(slot_dev)], axis=0)
    rest = jnp.concatenate([weights_ref[b] for b in range(slot_dev)], axis=0)
    terms = [ids.astype(jnp.bfloat16)]
    for _ in range(3):
        term = rest.astype(jnp.bfloat16)
        rest = rest - term.astype(jnp.float32)
        terms.append(term)
    at = lax.broadcasted_iota(jnp.int32, (TOP, WIDE - D), 0)
    lane = lax.broadcasted_iota(jnp.int32, (TOP, WIDE - D), 1)
    routing = sum(
        jnp.dot(
            term,
            jnp.where(lane == at + TOP * index, 1.0, 0.0).astype(jnp.bfloat16),
            preferred_element_type=jnp.float32,
        )
        for index, term in enumerate(terms)
    )
    row = jnp.concatenate([hidden, routing], axis=1)
    tokens_ref[...] = jnp.concatenate([row] * LINE, axis=0).astype(jnp.bfloat16)
    row = jnp.where(group == 0, assign_ref[0:1, :], assign_ref[1:2, :])
    tail = jnp.concatenate(
        [
            scale_ref[...].astype(jnp.float32),
            jnp.zeros((ROW - LAT - ROPE - LAT // QB, requests), jnp.float32),
        ],
        axis=0,
    ).astype(jnp.bfloat16)
    stored = jnp.concatenate([cache_ref[...], tail], axis=0)
    at = lax.broadcasted_iota(jnp.int32, (PLANE * KEEP, requests), 0)
    place, zh = at // KEEP, at % LINE
    slot = (place // FOUR * (LINE * FOUR) + zh * FOUR + place % FOUR) * slot_dev
    head = lax.broadcasted_iota(jnp.int32, (PLANE * KEEP, SIDE), 0) % KEEP < LINE
    for half, ref in ((group, kept_ref), (1 - group, given_ref)):
        choose = jnp.where(slot + half == row, 1.0, 0.0).astype(jnp.bfloat16)
        found = lax.dot_general(
            choose, stored, (((1,), (1,)), ((), ())), preferred_element_type=jnp.float32
        )
        tail = jnp.concatenate(
            [found[:, SIDE:], jnp.zeros((PLANE * KEEP, 2 * SIDE - ROW), jnp.float32)], axis=1
        )
        ref[...] = jnp.where(head, found[:, :SIDE], tail).astype(jnp.bfloat16)


def prepare(assign, cache, scale, hidden, ids, weights):
    tokens = LINE * hidden.shape[0] * STEPS
    args = (assign, cache, scale, hidden, ids, weights)
    shapes = ((PLANE * KEEP, SIDE), (PLANE * KEEP, SIDE), (tokens, WIDE))
    return pl.pallas_call(
        prepare_kernel,
        grid=(1,),
        out_shape=[jax.ShapeDtypeStruct(shape, jnp.bfloat16) for shape in shapes],
        in_specs=[whole(a.shape) for a in args],
        out_specs=[whole(shape) for shape in shapes],
        compiler_params=pltpu.CompilerParams(vmem_limit_bytes=58 * MIB),
        name="prepare",
    )(*args)


def finish_kernel(
    assign_ref, lengths_ref, gathered_ref, query_ref, fresh_ref, out_ref, moe_ref
):
    group, ep_index = lax.axis_index("pool"), lax.axis_index(EP_AXES)
    slot_dev, rows = query_ref.shape[:2]
    lines = gathered_ref.shape[0]
    parts = PLANE // SPREAD
    positions = parts * lines
    blocks = LAT // QB
    device = slot_dev * STEPS
    total = sum(
        gathered_ref[pl.ds(z * device, device), pl.ds(0, D)].astype(jnp.float32) for z in range(LINE)
    ).astype(jnp.bfloat16)
    for b in range(slot_dev):
        moe_ref[b] = total[b * STEPS : (b + 1) * STEPS]
    assigned = jnp.where(group == 0, assign_ref[1:2, :], assign_ref[0:1, :])
    lengths = jnp.where(group == 0, lengths_ref[1:2, :], lengths_ref[0:1, :])
    lane = lax.broadcasted_iota(jnp.int32, (rows, positions), 1)
    place = lane // lines * SPREAD + lane % SPREAD
    position = place // FOUR * (LINE * FOUR) + lane % lines // SPREAD * FOUR + place % FOUR
    new = 16
    step = lax.broadcasted_iota(jnp.int32, (rows, new), 0) // (rows // STEPS)
    token = lax.broadcasted_iota(jnp.int32, (rows, new), 1)
    by_rows = (((1,), (1,)), ((), ()))
    for b in range(slot_dev):
        slot = ep_index * slot_dev + b
        length = jnp.sum(jnp.where(assigned == slot, lengths, 0), axis=1, keepdims=True)
        keys = jnp.concatenate(
            [
                gathered_ref[:, pl.ds(D + (b * parts + part) * ROW, ROW)]
                for part in range(parts)
            ],
            axis=0,
        )
        scale = keys[:, LAT:].astype(jnp.float32).T[ROPE : ROPE + blocks]
        score = lax.dot_general(
            query_ref[b, :, pl.ds(LAT, ROPE)],
            keys[:, LAT : LAT + ROPE],
            by_rows,
            preferred_element_type=jnp.float32,
        )
        for n in range(blocks):
            part = lax.dot_general(
                query_ref[b, :, pl.ds(n * QB, QB)],
                keys[:, n * QB : (n + 1) * QB],
                by_rows,
                preferred_element_type=jnp.float32,
            )
            score = score + part * scale[n : n + 1]
        score = jnp.where(position < length, score * SCORE_SCALE, NEGATIVE)
        fresh = jnp.concatenate(
            [fresh_ref[b].astype(jnp.float32), jnp.zeros((new - STEPS, LAT + ROPE), jnp.float32)],
            axis=0,
        ).astype(jnp.bfloat16)
        score_fresh = lax.dot_general(
            query_ref[b], fresh, by_rows, preferred_element_type=jnp.float32
        )
        score_fresh = jnp.where(token <= step, score_fresh * SCORE_SCALE, NEGATIVE)
        top = jnp.maximum(
            jnp.max(score, axis=1, keepdims=True), jnp.max(score_fresh, axis=1, keepdims=True)
        )
        exp_cache, exp_fresh = jnp.exp(score - top), jnp.exp(score_fresh - top)
        summed = jnp.sum(exp_cache, axis=1, keepdims=True)
        summed = summed + jnp.sum(exp_fresh, axis=1, keepdims=True)
        prob = exp_cache / summed
        weight_fresh = (exp_fresh / summed).astype(jnp.bfloat16)
        for n in range(blocks):
            columns = slice(n * QB, (n + 1) * QB)
            weight = (prob * scale[n : n + 1]).astype(jnp.bfloat16)
            latent = jnp.dot(weight, keys[:, columns], preferred_element_type=jnp.float32)
            latent = latent + jnp.dot(
                weight_fresh, fresh[:, columns], preferred_element_type=jnp.float32
            )
            out_ref[b, :, pl.ds(n * QB, QB)] = latent.astype(jnp.bfloat16)


def finish(assign, lengths, gathered, queries, fresh):
    slot_dev, rows = queries.shape[:2]
    vmem = pl.BlockSpec(memory_space=pltpu.VMEM)
    return pl.pallas_call(
        finish_kernel,
        out_shape=(
            jax.ShapeDtypeStruct((slot_dev, rows, LAT), jnp.bfloat16),
            jax.ShapeDtypeStruct((slot_dev, STEPS, D), jnp.bfloat16),
        ),
        in_specs=[vmem] * 5,
        out_specs=(vmem, vmem),
        compiler_params=pltpu.CompilerParams(vmem_limit_bytes=16 * MIB),
        name="finish",
    )(assign, lengths, gathered, queries, fresh)


def on_device(
    cache,
    cache_scale,
    lengths,
    assign,
    queries,
    new_kv,
    hidden,
    expert_ids,
    expert_weights,
    gate_w,
    up_w,
    down_w,
):
    slot_dev, heads = queries.shape[1], queries.shape[3]
    token_count = slot_dev * STEPS
    kept, given, token_rows = prepare(
        assign,
        cache[0, :, 0, :].T,
        cache_scale[0, :, 0, :].T,
        hidden[0],
        expert_ids[0],
        expert_weights[0],
    )
    given = lax.ppermute(given, "pool", [(0, 1), (1, 0)])
    line = lax.all_to_all(
        token_rows.reshape(LINE, token_count, WIDE), LINE_AXES, 0, 0, tiled=True
    ).reshape(LINE * token_count, WIDE)
    line, given = lax.optimization_barrier((line, given))

    kept = pltpu.with_memory_space_constraint(kept, pltpu.HBM)
    sent, mix = dispatch(line, kept, given)
    taken = lax.all_to_all(
        sent.reshape(2 * PLANE, KEEP, D + SIDE), CROSS_AXES, 0, 0, tiled=True
    ).reshape(2 * PLANE * KEEP, D + SIDE)

    served = expert(taken, gate_w[0], up_w[0], down_w[0])

    served, taken = lax.optimization_barrier((served, taken))
    beside = turned(taken)
    served, beside = lax.optimization_barrier((served, beside))
    back = lax.all_to_all(
        served.reshape(2 * PLANE, KEEP, D), CROSS_AXES, 0, 0, tiled=True
    ).reshape(2 * PLANE * KEEP, D)

    mixed = combine(mix, back, beside)
    gathered = lax.all_to_all(
        mixed.reshape(LINE, token_count, -1), LINE_AXES, 0, 0, tiled=True
    ).reshape(mixed.shape)
    context, moe_out = finish(
        assign,
        lengths,
        gathered,
        queries[0].reshape(slot_dev, STEPS * heads, -1),
        new_kv[0],
    )
    return (
        context.reshape(1, slot_dev, STEPS, heads, LAT),
        moe_out.reshape(1, slot_dev, STEPS, D),
    )


def solution(mesh):
    fine = Mesh(
        mesh.devices.reshape(2, Y, XH, LINE, ZL, CORE), ("pool", "y", "xh", "zh", "zl", "core")
    )
    return jax.shard_map(
        on_device,
        mesh=fine,
        in_specs=(
            P("pool", None, EP_AXES, None),
            P("pool", None, EP_AXES, None),
            P(),
            P(),
            P("pool", EP_AXES, None, None, None),
            P("pool", EP_AXES, None, None),
            P("pool", EP_AXES, None, None),
            P("pool", EP_AXES, None, None),
            P("pool", EP_AXES, None, None),
            P(EP_AXES, None, "pool"),
            P(EP_AXES, None, "pool"),
            P(EP_AXES, "pool", None),
        ),
        out_specs=(P("pool", EP_AXES, None, None, None), P("pool", EP_AXES, None, None)),
        check_vma=False,
    )
```

```python
import jax
import jax.numpy as jnp
from jax import lax
from jax.experimental import pallas as pl
from jax.experimental.pallas import tpu as pltpu
from jax.sharding import Mesh, PartitionSpec as P

STEPS = 4
LAT = 512
ROPE = 64
QB = 128
D = 3584
TOP = 8
CAP = 2

Y, XH, LINE, ZL, CORE = 4, 2, 4, 2, 2
FOUR = ZL * CORE
PLANE = Y * XH * FOUR
KEEP = LINE * CAP
ROW = 640
SIDE = 384
SPREAD = 8

SCORE_SCALE = 192.0 ** (-0.5)
NEGATIVE = -1e30

LINE_AXES = "zh"
CROSS_AXES = ("pool", "y", "xh", "zl", "core")
EP_AXES = ("y", "xh", "zh", "zl", "core")


WIDE = D + 128
BLOCK = 512
MIB = 1 << 20


def whole(shape):
    return pl.BlockSpec(shape, lambda i: (0,) * len(shape))


def dispatch_kernel(line_ref, kept_ref, given_ref, sent_ref, mix_ref, done):
    group, zh = lax.axis_index("pool"), lax.axis_index(LINE_AXES)
    count = PLANE * KEEP
    copies = []
    for index, (half, ref) in enumerate(((group, given_ref), (1 - group, kept_ref))):
        top = pl.multiple_of(half * count, count)
        target = sent_ref.at[pl.ds(top, count), pl.ds(D, SIDE)]
        copies.append(pltpu.make_async_copy(ref, target, done.at[index]))
        copies[index].start()
    tokens = line_ref.shape[0]
    routing = jnp.concatenate(
        [line_ref[:, pl.ds(D, 128)].astype(jnp.float32), jnp.zeros((128 - tokens, 128), jnp.float32)],
        axis=0,
    ).T[:, :tokens]
    place = lax.broadcasted_iota(jnp.int32, (PLANE, tokens), 0)
    expert_at = place // FOUR * (LINE * FOUR) + zh * FOUR + place % FOUR
    hit = jnp.zeros((PLANE, tokens), jnp.float32)
    share = jnp.zeros((PLANE, tokens), jnp.float32)
    for k in range(TOP):
        weight = sum(routing[TOP * part + k : TOP * part + k + 1] for part in (1, 2, 3))
        named = routing[k : k + 1].astype(jnp.int32) == expert_at
        hit = hit + jnp.where(named, 1.0, 0.0)
        share = share + jnp.where(named, weight, 0.0)
    token = lax.broadcasted_iota(jnp.int32, (tokens, tokens), 0)
    other = lax.broadcasted_iota(jnp.int32, (tokens, tokens), 1)
    rank = jnp.dot(
        hit.astype(jnp.bfloat16),
        jnp.where(token < other, 1.0, 0.0).astype(jnp.bfloat16),
        preferred_element_type=jnp.float32,
    )
    rank = jnp.where(hit > 0.0, rank, -1.0).astype(jnp.int32)
    seat = lax.broadcasted_iota(jnp.int32, (KEEP, tokens), 0)
    chosen = [seat == rank[e : e + 1] for e in range(PLANE)]
    choose = jnp.concatenate([jnp.where(c, 1.0, 0.0) for c in chosen], axis=0)
    choose = choose.astype(jnp.bfloat16)
    mix = jnp.concatenate(
        [jnp.where(chosen[e], share[e : e + 1], 0.0) for e in range(PLANE)], axis=0
    )
    high = mix.astype(jnp.bfloat16)
    low = (mix - high.astype(jnp.float32)).astype(jnp.bfloat16)
    same = jnp.where(token == other, 1.0, 0.0).astype(jnp.bfloat16)
    for index, part in enumerate((high, low)):
        across = lax.dot_general(
            same, part, (((1,), (1,)), ((), ())), preferred_element_type=jnp.float32
        ).astype(jnp.bfloat16)
        mix_ref[index] = jnp.concatenate([across, across], axis=1)
    for start in range(0, D, BLOCK):
        columns = pl.ds(start, BLOCK)
        rows = jnp.dot(choose, line_ref[:, columns], preferred_element_type=jnp.float32)
        rows = rows.astype(jnp.bfloat16)
        sent_ref[pl.ds(0, count), columns] = rows
        sent_ref[pl.ds(count, count), columns] = rows
    for copy in copies:
        copy.wait()


def dispatch(line, kept, given):
    tokens = line.shape[0]
    count = 2 * PLANE * KEEP
    vmem = pl.BlockSpec(memory_space=pltpu.VMEM)
    return pl.pallas_call(
        dispatch_kernel,
        out_shape=(
            jax.ShapeDtypeStruct((count, D + SIDE), jnp.bfloat16),
            jax.ShapeDtypeStruct((2, tokens, count), jnp.bfloat16),
        ),
        in_specs=[vmem, pl.BlockSpec(memory_space=pltpu.HBM), pl.BlockSpec(memory_space=pl.ANY)],
        out_specs=(vmem, vmem),
        scratch_shapes=[pltpu.SemaphoreType.DMA((2,))],
        compiler_params=pltpu.CompilerParams(vmem_limit_bytes=24 * MIB),
        cost_estimate=pl.CostEstimate(
            flops=2 * count * tokens * D, bytes_accessed=8 * count * D, transcendentals=0
        ),
        name="dispatch",
    )(line, kept, given)


def rows_of(count):
    return count // (SPREAD * KEEP)


def turn_kernel(one_ref, two_ref, three_ref, out_ref):
    rows = out_ref.shape[0]
    group = SPREAD * KEEP
    to = lax.broadcasted_iota(jnp.int32, (rows, group), 0)
    at = lax.broadcasted_iota(jnp.int32, (rows, group), 1)
    first = to % SPREAD * KEEP + to // SPREAD
    blocks = rows_of(one_ref.shape[0])
    out_ref[:, pl.ds(blocks * (LAT + ROPE), 128)] = jnp.zeros((rows, 128), jnp.bfloat16)
    for index in range(blocks):
        block = pl.ds(index * group, group)
        three = jnp.concatenate([r[block, :] for r in (one_ref, two_ref, three_ref)], axis=1)
        for part, width in enumerate((SIDE, ROW - SIDE)):
            turn = jnp.where(at == first + part * LINE, 1.0, 0.0).astype(jnp.bfloat16)
            moved = jnp.dot(turn, three[:, :width], preferred_element_type=jnp.float32)
            moved = moved.astype(jnp.bfloat16)
            if part == 0:
                out_ref[:, pl.ds(index * LAT, SIDE)] = moved
            else:
                rest, scales = LAT - SIDE, LAT // QB
                out_ref[:, pl.ds(index * LAT + SIDE, rest)] = moved[:, :rest]
                out_ref[:, pl.ds(blocks * LAT + index * ROPE, ROPE)] = moved[:, rest : rest + ROPE]
                out_ref[:, pl.ds(blocks * (LAT + ROPE) + index * scales, scales)] = moved[
                    :, rest + ROPE : rest + ROPE + scales
                ]


def turned(taken):
    rows = taken.shape[0]
    shape = (LINE * SPREAD, rows_of(rows) * (LAT + ROPE) + 128)
    return pl.pallas_call(
        turn_kernel,
        grid=(1,),
        out_shape=jax.ShapeDtypeStruct(shape, jnp.bfloat16),
        in_specs=[
            pl.BlockSpec((rows, 128), lambda i, at=at: (0, D // 128 + at)) for at in range(3)
        ],
        out_specs=whole(shape),
        compiler_params=pltpu.CompilerParams(vmem_limit_bytes=12 * MIB),
        name="turned",
    )(taken, taken, taken)


def inner_kernel(taken_ref, gate_ref, up_ref, inner_ref):
    for start in range(0, inner_ref.shape[1], 256):
        columns = pl.ds(start, 256)
        rows = taken_ref[:, pl.ds(0, D)]
        gate = jnp.dot(rows, gate_ref[:, columns], preferred_element_type=jnp.float32)
        up = jnp.dot(rows, up_ref[:, columns], preferred_element_type=jnp.float32)
        inner_ref[:, columns] = (jax.nn.silu(gate) * up).astype(jnp.bfloat16)


def served_kernel(inner_ref, down_ref, out_ref):
    for start in range(0, D, BLOCK):
        columns = pl.ds(start, BLOCK)
        out_ref[:, columns] = jnp.dot(
            inner_ref[...], down_ref[:, columns], preferred_element_type=jnp.float32
        ).astype(jnp.bfloat16)


def expert(taken, gate, up, down):
    count, width = taken.shape[0], gate.shape[1]
    vmem = pl.BlockSpec(memory_space=pltpu.VMEM)
    inner = pl.pallas_call(
        inner_kernel,
        out_shape=jax.ShapeDtypeStruct((count, width), jnp.bfloat16),
        in_specs=[vmem, vmem, vmem],
        out_specs=vmem,
        compiler_params=pltpu.CompilerParams(vmem_limit_bytes=20 * MIB),
        cost_estimate=pl.CostEstimate(
            flops=4 * count * width * D,
            bytes_accessed=4 * width * D + 2 * count * (D + width),
            transcendentals=count * width,
        ),
        name="inner",
    )(taken, gate, up)
    return pl.pallas_call(
        served_kernel,
        out_shape=jax.ShapeDtypeStruct((count, D), jnp.bfloat16),
        in_specs=[vmem, vmem],
        out_specs=vmem,
        compiler_params=pltpu.CompilerParams(vmem_limit_bytes=16 * MIB),
        cost_estimate=pl.CostEstimate(
            flops=2 * count * width * D,
            bytes_accessed=2 * width * D + 2 * count * (D + width),
            transcendentals=0,
        ),
        name="served",
    )(inner, down)


def combine_kernel(mix_ref, back_ref, beside_ref, out_ref):
    tokens = mix_ref.shape[1]
    mix = jnp.concatenate([mix_ref[0], mix_ref[1]], axis=0)
    for start in range(0, D, BLOCK):
        columns = pl.ds(start, BLOCK)
        both = jnp.dot(mix, back_ref[:, columns], preferred_element_type=jnp.float32)
        out_ref[:, columns] = (both[:tokens] + both[tokens:]).astype(jnp.bfloat16)
    out_ref[:, pl.ds(D, beside_ref.shape[1])] = beside_ref[...]


def combine(mix, back, beside):
    vmem = pl.BlockSpec(memory_space=pltpu.VMEM)
    return pl.pallas_call(
        combine_kernel,
        out_shape=jax.ShapeDtypeStruct((mix.shape[1], D + beside.shape[1]), jnp.bfloat16),
        in_specs=[vmem, vmem, vmem],
        out_specs=vmem,
        compiler_params=pltpu.CompilerParams(vmem_limit_bytes=12 * MIB),
        name="combine",
    )(mix, back, beside)


def prepare_kernel(
    assign_ref, cache_ref, scale_ref, hidden_ref, ids_ref, weights_ref,
    kept_ref, given_ref, tokens_ref,
):
    group = lax.axis_index("pool")
    slot_dev = hidden_ref.shape[0]
    requests = assign_ref.shape[1]
    hidden = [hidden_ref[b].astype(jnp.float32) for b in range(slot_dev)]
    hidden = jnp.concatenate(hidden, axis=0)
    ids = jnp.concatenate([ids_ref[b].astype(jnp.float32) for b in range(slot_dev)], axis=0)
    rest = jnp.concatenate([weights_ref[b] for b in range(slot_dev)], axis=0)
    terms = [ids.astype(jnp.bfloat16)]
    for _ in range(3):
        term = rest.astype(jnp.bfloat16)
        rest = rest - term.astype(jnp.float32)
        terms.append(term)
    at = lax.broadcasted_iota(jnp.int32, (TOP, WIDE - D), 0)
    lane = lax.broadcasted_iota(jnp.int32, (TOP, WIDE - D), 1)
    routing = sum(
        jnp.dot(
            term,
            jnp.where(lane == at + TOP * index, 1.0, 0.0).astype(jnp.bfloat16),
            preferred_element_type=jnp.float32,
        )
        for index, term in enumerate(terms)
    )
    row = jnp.concatenate([hidden, routing], axis=1)
    tokens_ref[...] = jnp.concatenate([row] * LINE, axis=0).astype(jnp.bfloat16)
    row = jnp.where(group == 0, assign_ref[0:1, :], assign_ref[1:2, :])
    tail = jnp.concatenate(
        [
            scale_ref[...].astype(jnp.float32),
            jnp.zeros((ROW - LAT - ROPE - LAT // QB, requests), jnp.float32),
        ],
        axis=0,
    ).astype(jnp.bfloat16)
    stored = jnp.concatenate([cache_ref[...], tail], axis=0)
    at = lax.broadcasted_iota(jnp.int32, (PLANE * KEEP, requests), 0)
    place, zh = at // KEEP, at % LINE
    slot = (place // FOUR * (LINE * FOUR) + zh * FOUR + place % FOUR) * slot_dev
    head = lax.broadcasted_iota(jnp.int32, (PLANE * KEEP, SIDE), 0) % KEEP < LINE
    for half, ref in ((group, kept_ref), (1 - group, given_ref)):
        choose = jnp.where(slot + half == row, 1.0, 0.0).astype(jnp.bfloat16)
        found = lax.dot_general(
            choose, stored, (((1,), (1,)), ((), ())), preferred_element_type=jnp.float32
        )
        tail = jnp.concatenate(
            [found[:, SIDE:], jnp.zeros((PLANE * KEEP, 2 * SIDE - ROW), jnp.float32)], axis=1
        )
        ref[...] = jnp.where(head, found[:, :SIDE], tail).astype(jnp.bfloat16)


def prepare(assign, cache, scale, hidden, ids, weights):
    tokens = LINE * hidden.shape[0] * STEPS
    args = (assign, cache, scale, hidden, ids, weights)
    shapes = ((PLANE * KEEP, SIDE), (PLANE * KEEP, SIDE), (tokens, WIDE))
    return pl.pallas_call(
        prepare_kernel,
        grid=(1,),
        out_shape=[jax.ShapeDtypeStruct(shape, jnp.bfloat16) for shape in shapes],
        in_specs=[whole(a.shape) for a in args],
        out_specs=[whole(shape) for shape in shapes],
        compiler_params=pltpu.CompilerParams(vmem_limit_bytes=58 * MIB),
        name="prepare",
    )(*args)


def finish_kernel(
    assign_ref, lengths_ref, gathered_ref, query_ref, fresh_ref, out_ref, moe_ref
):
    group, ep_index = lax.axis_index("pool"), lax.axis_index(EP_AXES)
    slot_dev, rows = query_ref.shape[:2]
    lines = gathered_ref.shape[0]
    parts = PLANE // SPREAD
    positions = parts * lines
    blocks = LAT // QB
    device = slot_dev * STEPS
    total = sum(
        gathered_ref[pl.ds(z * device, device), pl.ds(0, D)].astype(jnp.float32) for z in range(LINE)
    ).astype(jnp.bfloat16)
    for b in range(slot_dev):
        moe_ref[b] = total[b * STEPS : (b + 1) * STEPS]
    assigned = jnp.where(group == 0, assign_ref[1:2, :], assign_ref[0:1, :])
    lengths = jnp.where(group == 0, lengths_ref[1:2, :], lengths_ref[0:1, :])
    lane = lax.broadcasted_iota(jnp.int32, (rows, positions), 1)
    place = lane // lines * SPREAD + lane % SPREAD
    position = place // FOUR * (LINE * FOUR) + lane % lines // SPREAD * FOUR + place % FOUR
    new = 16
    step = lax.broadcasted_iota(jnp.int32, (rows, new), 0) // (rows // STEPS)
    token = lax.broadcasted_iota(jnp.int32, (rows, new), 1)
    by_rows = (((1,), (1,)), ((), ()))
    scales = gathered_ref[:, pl.ds(D + slot_dev * parts * (LAT + ROPE), 128)]
    scales = scales.astype(jnp.float32).T
    for b in range(slot_dev):
        slot = ep_index * slot_dev + b
        length = jnp.sum(jnp.where(assigned == slot, lengths, 0), axis=1, keepdims=True)
        held = [b * parts + part for part in range(parts)]
        every = slot_dev * parts
        keys = jnp.concatenate(
            [gathered_ref[:, pl.ds(D + at * LAT, LAT)] for at in held], axis=0
        )
        ropes = jnp.concatenate(
            [gathered_ref[:, pl.ds(D + every * LAT + at * ROPE, ROPE)] for at in held], axis=0
        )
        scale = jnp.concatenate([scales[at * blocks : (at + 1) * blocks] for at in held], axis=1)
        score = lax.dot_general(
            query_ref[b, :, pl.ds(LAT, ROPE)],
            ropes,
            by_rows,
            preferred_element_type=jnp.float32,
        )
        for n in range(blocks):
            part = lax.dot_general(
                query_ref[b, :, pl.ds(n * QB, QB)],
                keys[:, n * QB : (n + 1) * QB],
                by_rows,
                preferred_element_type=jnp.float32,
            )
            score = score + part * scale[n : n + 1]
        score = jnp.where(position < length, score * SCORE_SCALE, NEGATIVE)
        fresh = jnp.concatenate(
            [fresh_ref[b].astype(jnp.float32), jnp.zeros((new - STEPS, LAT + ROPE), jnp.float32)],
            axis=0,
        ).astype(jnp.bfloat16)
        score_fresh = lax.dot_general(
            query_ref[b], fresh, by_rows, preferred_element_type=jnp.float32
        )
        score_fresh = jnp.where(token <= step, score_fresh * SCORE_SCALE, NEGATIVE)
        top = jnp.maximum(
            jnp.max(score, axis=1, keepdims=True), jnp.max(score_fresh, axis=1, keepdims=True)
        )
        exp_cache, exp_fresh = jnp.exp(score - top), jnp.exp(score_fresh - top)
        summed = jnp.sum(exp_cache, axis=1, keepdims=True)
        summed = summed + jnp.sum(exp_fresh, axis=1, keepdims=True)
        prob = exp_cache / summed
        weight_fresh = (exp_fresh / summed).astype(jnp.bfloat16)
        for n in range(blocks):
            columns = slice(n * QB, (n + 1) * QB)
            weight = (prob * scale[n : n + 1]).astype(jnp.bfloat16)
            latent = jnp.dot(weight, keys[:, columns], preferred_element_type=jnp.float32)
            latent = latent + jnp.dot(
                weight_fresh, fresh[:, columns], preferred_element_type=jnp.float32
            )
            out_ref[b, :, pl.ds(n * QB, QB)] = latent.astype(jnp.bfloat16)


def finish(assign, lengths, gathered, queries, fresh):
    slot_dev, rows = queries.shape[:2]
    vmem = pl.BlockSpec(memory_space=pltpu.VMEM)
    return pl.pallas_call(
        finish_kernel,
        out_shape=(
            jax.ShapeDtypeStruct((slot_dev, rows, LAT), jnp.bfloat16),
            jax.ShapeDtypeStruct((slot_dev, STEPS, D), jnp.bfloat16),
        ),
        in_specs=[vmem] * 5,
        out_specs=(vmem, vmem),
        compiler_params=pltpu.CompilerParams(vmem_limit_bytes=16 * MIB),
        name="finish",
    )(assign, lengths, gathered, queries, fresh)


def on_device(
    cache,
    cache_scale,
    lengths,
    assign,
    queries,
    new_kv,
    hidden,
    expert_ids,
    expert_weights,
    gate_w,
    up_w,
    down_w,
):
    slot_dev, heads = queries.shape[1], queries.shape[3]
    token_count = slot_dev * STEPS
    kept, given, token_rows = prepare(
        assign,
        cache[0, :, 0, :].T,
        cache_scale[0, :, 0, :].T,
        hidden[0],
        expert_ids[0],
        expert_weights[0],
    )
    given = lax.ppermute(given, "pool", [(0, 1), (1, 0)])
    line = lax.all_to_all(
        token_rows.reshape(LINE, token_count, WIDE), LINE_AXES, 0, 0, tiled=True
    ).reshape(LINE * token_count, WIDE)
    line, given = lax.optimization_barrier((line, given))

    kept = pltpu.with_memory_space_constraint(kept, pltpu.HBM)
    sent, mix = dispatch(line, kept, given)
    taken = lax.all_to_all(
        sent.reshape(2 * PLANE, KEEP, D + SIDE), CROSS_AXES, 0, 0, tiled=True
    ).reshape(2 * PLANE * KEEP, D + SIDE)

    served = expert(taken, gate_w[0], up_w[0], down_w[0])

    served, taken = lax.optimization_barrier((served, taken))
    beside = turned(taken)
    served, beside = lax.optimization_barrier((served, beside))
    back = lax.all_to_all(
        served.reshape(2 * PLANE, KEEP, D), CROSS_AXES, 0, 0, tiled=True
    ).reshape(2 * PLANE * KEEP, D)

    mixed = combine(mix, back, beside)
    gathered = lax.all_to_all(
        mixed.reshape(LINE, token_count, -1), LINE_AXES, 0, 0, tiled=True
    ).reshape(mixed.shape)
    context, moe_out = finish(
        assign,
        lengths,
        gathered,
        queries[0].reshape(slot_dev, STEPS * heads, -1),
        new_kv[0],
    )
    return (
        context.reshape(1, slot_dev, STEPS, heads, LAT),
        moe_out.reshape(1, slot_dev, STEPS, D),
    )


def solution(mesh):
    fine = Mesh(
        mesh.devices.reshape(2, Y, XH, LINE, ZL, CORE), ("pool", "y", "xh", "zh", "zl", "core")
    )
    return jax.shard_map(
        on_device,
        mesh=fine,
        in_specs=(
            P("pool", None, EP_AXES, None),
            P("pool", None, EP_AXES, None),
            P(),
            P(),
            P("pool", EP_AXES, None, None, None),
            P("pool", EP_AXES, None, None),
            P("pool", EP_AXES, None, None),
            P("pool", EP_AXES, None, None),
            P("pool", EP_AXES, None, None),
            P(EP_AXES, None, "pool"),
            P(EP_AXES, None, "pool"),
            P(EP_AXES, "pool", None),
        ),
        out_specs=(P("pool", EP_AXES, None, None, None), P("pool", EP_AXES, None, None)),
        check_vma=False,
    )
```
